32 devices in a mesh: dp: 2 (over x), expert: 4 (over z), tensor: 4 (over y, core).
Axes of the slice: x: 2, y: 2, z: 4, core: 2. Of those that a mesh axis runs over, the one named last changes fastest.
Arguments:
- tokens: bfloat16 [3840, 1536], P(('dp', 'expert')), may hold values from -6 to 6
- out_cotangent: bfloat16 [3840, 1536], P(('dp', 'expert')), may hold values from -6 to 6
- first_gain: bfloat16 [1536], replicated, may hold values from 0.5 to 1.5
- query_weight: bfloat16 [1536, 1536], P(None, 'tensor'), may hold values from -0.15625 to 0.15625
- key_value_matrix: bfloat16 [1536, 1024], P(None, 'tensor'), may hold values from -0.15625 to 0.15625
- output_weight: bfloat16 [1536, 1536], P('tensor'), may hold values from -1.25 to 1.25
- second_gain: bfloat16 [1536], replicated, may hold values from 0.5 to 1.5
- expert_gate_up: bfloat16 [40, 1536, 1024], P('expert', None, 'tensor'), may hold values from -0.15625 to 0.15625
- expert_down: bfloat16 [40, 512, 1536], P('expert', 'tensor'), may hold values from -1 to 1
- routes: int32 [3840, 8], P(('dp', 'expert')), may hold values from 0 to 39, all different within a row; in each aligned block of 480 rows (0 to 479, 480 to 959, ...) at most 192 rows name the same one
- route_gates: float32 [3840, 8], P(('dp', 'expert')), may hold values from 0 to 1, as said below
- expert_slot: int32 [40], replicated, may hold values from 0 to 39, each once
- parent_segments: int32 [2, 7], P('dp'), may hold values from 0 to 6, as said below
- token_segments: int32 [3840], P('dp'), may hold values from 0 to 6, as said below
Outputs:
- layer_output: bfloat16 [3840, 1536], P(('dp', 'expert'))
- input_gradient: bfloat16 [3840, 1536], P(('dp', 'expert'))
- first_gain_gradient: float32 [1536], replicated
- query_gradient: float32 [1536, 1536], P(None, 'tensor')
- key_value_gradient: float32 [1536, 1024], P(None, 'tensor')
- output_gradient: float32 [1536, 1536], P('tensor')
- second_gain_gradient: float32 [1536], replicated
- expert_gate_up_gradient: float32 [40, 1536, 1024], P('expert', None, 'tensor')
- expert_down_gradient: float32 [40, 512, 1536], P('expert', 'tensor')
The draws below stay inside these ranges and needn't reach their ends.
Inputs may be any that keep to these rules, and one draw needn't show every extreme that they name: `routes`: each row names 8 different experts. Among the 480 rows of one device no expert is named more than 192 times, and in every draw some device names some expert exactly 192 times. `route_gates`: Positive; each row sums to 1. A permutation of the experts. Expert e's weights are entry expert_slot[e] of the expert arrays. `parent_segments`: each tree has 7 segments: one root, which is its own parent, with two children, each of which has two leaf children. `token_segments`: the root holds 640 tokens, its children 2 * 160 each, the leaves 160 each. A segment's tokens are contiguous and come after those of its parent.
All inputs are finite; a program needn't handle non-finite values.
Results may differ from the reference program's by a relative error of at most 0.025.
Values may be sent and summed in bfloat16 or wider, within the bound.
No kernel may reach another device: no remote copies, remote signals or barrier semaphores. Data moves between devices by JAX's collectives and lax.ppermute only.
A program may use at most 384 MiB of HBM per device.

```python
import math
import jax
import jax.numpy as jnp
import numpy as np
from jax import lax

MODEL_DIMENSION = 1536
QUERY_HEADS = 24
KEY_VALUE_HEADS = 8
HEAD_SIZE = 64
FF = 512
EXPERTS = 40
TOP = 8
PAIR = 64
SEGS = 7
TOK_DEV = 480
CAP = 192
LEAF = 160
TREE_TOKENS = 1920
TOKEN_TOTAL = 3840
N_DP = 2
N_TENSOR = 4


def arrangements(members):
    if len(members) == 0:
        return [[]]
    result = []
    for position in range(len(members)):
        remaining = members[:position] + members[position + 1:]
        for suffix in arrangements(remaining):
            result.append([members[position]] + suffix)
    return result


def tree_draw(key):
    tree_parent = [0, 0, 0, 1, 1, 2, 2]
    layouts = []
    for candidate in arrangements([1, 2, 3, 4, 5, 6]):
        layout_order = [0] + candidate
        if all((layout_order.index(tree_parent[segment]) < layout_order.index(segment) for segment in layout_order[1:])):
            layouts.append(layout_order)
    layout_table = jnp.asarray(np.array(layouts, dtype=np.int32))
    node_lengths = jnp.asarray(np.array([4, 2, 2, 1, 1, 1, 1], dtype=np.int32)) * LEAF
    parent_table = jnp.asarray(np.array(tree_parent, dtype=np.int32))
    node_range = jnp.arange(SEGS, dtype=jnp.int32)
    parent_rows = []
    segment_rows = []
    for which_tree_index in range(TOKEN_TOTAL // TREE_TOKENS):
        tree_key = jax.random.fold_in(key, which_tree_index)
        choose_key, label_key, inner_key = jax.random.split(tree_key, 3)
        chosen = jax.random.randint(choose_key, (), 0, layout_table.shape[0])
        layout_order = layout_table[chosen]
        shuffled = jax.random.permutation(label_key, SEGS).astype(jnp.int32)
        top_place = jnp.sum(jnp.where(shuffled == SEGS - 1, node_range, 0)).astype(jnp.int32)
        inner_place = jax.random.randint(inner_key, (), 0, 3).astype(jnp.int32)
        moved_label = jnp.sum(jnp.where(node_range == inner_place, shuffled, 0)).astype(jnp.int32)
        labels = jnp.where(node_range == inner_place, SEGS - 1, jnp.where(node_range == top_place, moved_label, shuffled)).astype(jnp.int32)
        laid_lengths = node_lengths[layout_order]
        starts = jnp.cumsum(laid_lengths) - laid_lengths
        row_index = jnp.arange(TREE_TOKENS, dtype=jnp.int32)
        slot_place = jnp.sum((row_index[:, None] >= starts[None, 1:]).astype(jnp.int32), axis=1)
        segment_rows.append(labels[layout_order[slot_place]])
        parent_rows.append(jnp.zeros((SEGS,), jnp.int32).at[labels].set(labels[parent_table]))
    return (jnp.stack(parent_rows), jnp.concatenate(segment_rows))


def draw_parent_segments(key, part):
    shared = tree_draw(key)
    return shared[0]


def draw_token_segments(key, part):
    shared = tree_draw(key)
    return shared[1]


def draw_route_gates(key, part):
    key = jax.random.fold_in(key, 11)
    logits = 0.5 * jax.random.normal(key, (TOKEN_TOTAL, TOP), jnp.float32)
    return jax.nn.softmax(logits, axis=-1)


def block_scale(stream_key, extent, cuts, smallest, top_value):
    loudness, own = 1.0, jax.random.fold_in(stream_key, 6)
    for dim, parts in cuts:
        heights = jnp.exp(jax.random.uniform(jax.random.fold_in(own, dim), (parts,), jnp.float32, smallest / len(cuts), top_value / len(cuts)))
        loudness = loudness * jnp.repeat(heights, extent[dim] // parts).reshape([-1 if axis == dim else 1 for axis in range(len(extent))])
    return loudness


def shared_out(stream_key, own, number, rows, amount, top, reach, skew):
    ranking = jax.random.permutation(stream_key, amount)
    crowded, ordinary = portions_of(amount, rows * top, reach, skew, True), portions_of(amount, rows * top, reach, skew, False)
    places = jnp.arange(amount)

    def named(sizes, rotation):
        used = int((sizes > 0).sum())
        fixed = max(1, used // 4)
        moved = fixed + (places - fixed + rotation * (used - fixed)) % max(1, amount - fixed)
        return jnp.zeros((amount,), jnp.int32).at[ranking[jnp.where(places < fixed, places, moved)]].set(jnp.asarray(sizes, jnp.int32))

    sizes = jnp.where(number % 4 == 0, named(crowded, number // 4), named(ordinary, number - number // 4 - 1))
    mixed = jax.random.permutation(jax.random.fold_in(own, 3), amount)
    donor, sink = mixed[0:amount // 2 * 2:2], mixed[1:amount // 2 * 2:2]
    room = jnp.minimum(sizes[donor] - 1, reach - sizes[sink]) // 2
    room = jnp.where((donor == ranking[0]) | (sink == ranking[0]) | (sizes[sink] == 0), 0, jnp.maximum(room, 0))
    moved = jax.random.randint(jax.random.fold_in(own, 4), (amount // 2,), 0, 1 << 20) % (room + 1)
    sizes = sizes.at[donor].add(-moved).at[sink].add(moved)
    items = jnp.searchsorted(jnp.cumsum(sizes), jnp.arange(rows * top), side="right").astype(jnp.int32)
    grid = items.reshape(top, rows).T
    grid = grid[jax.random.permutation(jax.random.fold_in(own, 1), rows)]
    rotation = jax.random.randint(jax.random.fold_in(own, 2), (rows, 1), 0, top)
    return jnp.take_along_axis(grid, (jnp.arange(top)[None, :] + rotation) % top, axis=1)


def portions_of(count, total, bound, skew, full):
    loads = [(1 << 20) // math.isqrt(rank ** skew) + 1 for rank in range(1, count + 1)]
    largest = bound if full else min(bound, max(-(-total // count), total * loads[0] // sum(loads)))
    least = 1 if total - largest >= count - 1 else 0
    counts, surplus = [largest] + [least] * (count - 1), total - largest - least * (count - 1)
    while surplus > 0:
        free = [i for i in range(1, count) if counts[i] < largest] or [i for i in range(1, count) if counts[i] < bound]
        mass, left = sum([loads[i] for i in free]), surplus
        for i in free:
            more = min(bound - counts[i], max(1, left * loads[i] // mass), surplus)
            counts[i] = counts[i] + more
            surplus = surplus - more
    return np.array(counts)


def normal_values(rng, extent, spread, limit, shards=(), held_as=jnp.bfloat16):
    loudness = block_scale(rng, extent, shards, -0.22, 0.18) if shards else 1.0
    values = jax.random.normal(rng, extent, jnp.float32) * spread * loudness
    return jnp.minimum(jnp.maximum(values, -limit), limit).astype(held_as)


def setup_inputs(seed: int = 0) -> dict:
    arg_keys = jax.random.split(jax.random.key(seed), 15)
    tokens = normal_values(arg_keys[0], (TOKEN_TOTAL, MODEL_DIMENSION), 1.0, 6.0, ((0, 8),))
    out_cotangent = normal_values(arg_keys[1], (TOKEN_TOTAL, MODEL_DIMENSION), 1.0, 6.0, ((0, 8),))
    first_gain = jnp.clip(1.0 + 0.1 * jax.random.normal(arg_keys[2], (MODEL_DIMENSION,), jnp.float32), 0.5, 1.5).astype(jnp.bfloat16)
    query_weight = normal_values(arg_keys[3], (MODEL_DIMENSION, QUERY_HEADS * HEAD_SIZE), MODEL_DIMENSION ** -0.5, 0.15625, ((1, 4),))
    key_value_matrix = normal_values(arg_keys[4], (MODEL_DIMENSION, 2 * KEY_VALUE_HEADS * HEAD_SIZE), MODEL_DIMENSION ** -0.5, 0.15625, ((1, 4),))
    output_weight = normal_values(arg_keys[5], (QUERY_HEADS * HEAD_SIZE, MODEL_DIMENSION), (QUERY_HEADS * HEAD_SIZE // 64) ** -0.5, 1.25, ((0, 4),))
    second_gain = jnp.clip(1.0 + 0.1 * jax.random.normal(arg_keys[6], (MODEL_DIMENSION,), jnp.float32), 0.5, 1.5).astype(jnp.bfloat16)
    expert_gate_up = normal_values(arg_keys[7], (EXPERTS, MODEL_DIMENSION, 2 * FF), MODEL_DIMENSION ** -0.5, 0.15625, ((0, 4), (2, 4)))
    expert_down = normal_values(arg_keys[8], (EXPERTS, FF, MODEL_DIMENSION), (FF // 16) ** -0.5, 1.0, ((0, 4), (1, 4)))
    routes_keys = jax.random.split(jax.random.fold_in(arg_keys[9], 1), TOKEN_TOTAL // TOK_DEV)
    routes_turns = jax.random.permutation(jax.random.fold_in(arg_keys[9], 3), TOKEN_TOTAL // TOK_DEV)
    routes = jax.vmap(lambda own, number: shared_out(jax.random.fold_in(arg_keys[9], 2), own, number, TOK_DEV, EXPERTS, TOP, CAP, 1))(routes_keys, routes_turns).reshape((TOKEN_TOTAL, TOP))
    route_gates = draw_route_gates(jax.random.fold_in(arg_keys[14], 71), 0)
    expert_slot = jax.random.permutation(arg_keys[11], EXPERTS).astype(jnp.int32)
    parent_segments = draw_parent_segments(jax.random.fold_in(arg_keys[14], 71), 0)
    token_segments = draw_token_segments(jax.random.fold_in(arg_keys[14], 71), 0)
    return {"tokens": tokens, "out_cotangent": out_cotangent, "first_gain": first_gain, "query_weight": query_weight, "key_value_matrix": key_value_matrix, "output_weight": output_weight, "second_gain": second_gain, "expert_gate_up": expert_gate_up, "expert_down": expert_down, "routes": routes, "route_gates": route_gates, "expert_slot": expert_slot, "parent_segments": parent_segments, "token_segments": token_segments}


EPS = 1e-05
EXACT_PRECISION = lax.Precision.HIGHEST

@jax.custom_vjp
def low(v):
    return lax.optimization_barrier(v.astype(jnp.bfloat16)).astype(jnp.float32)

@jax.custom_vjp
def reduced_precision_backward(v):
    return v

def low_keep(v):
    return (low(v), None)

def low_pass(kept, grad):
    return (grad,)

def back_keep(v):
    return (v, None)

def back_low(kept, grad):
    return (low(grad),)
low.defvjp(low_keep, low_pass)
reduced_precision_backward.defvjp(back_keep, back_low)

def normalize(values, gain_vector):
    inverse_rms = lax.rsqrt(lax.optimization_barrier(jnp.mean(values * values, axis=-1, keepdims=True)) + EPS)
    return values * inverse_rms * gain_vector

def rotate(values, position):
    half_width = values.shape[-1] // 2
    frequency = jnp.power(10000.0, -jnp.arange(half_width, dtype=jnp.float32) / half_width)
    angles = position.astype(jnp.float32)[:, None] * frequency[None, :]
    cosine = jnp.cos(angles)[:, None, :]
    sine_part = jnp.sin(angles)[:, None, :]
    first_half = values[..., :half_width]
    second_half = values[..., half_width:]
    return jnp.concatenate([first_half * cosine - second_half * sine_part, second_half * cosine + first_half * sine_part], axis=-1)

def swiglu(gate_part, up_part):
    return gate_part * jax.nn.sigmoid(gate_part) * up_part

def split_pairs(hidden, pair_width):
    leading = hidden.shape[:-1]
    width = hidden.shape[-1] // 2
    grouped = hidden.reshape(leading + (width // pair_width, 2, pair_width))
    return (grouped[..., 0, :].reshape(leading + (width,)), grouped[..., 1, :].reshape(leading + (width,)))

def tree_layout(parents, segments):
    labels = jnp.arange(parents.shape[0], dtype=jnp.int32)
    up_two = lax.optimization_barrier(jnp.sum((parents[:, None] == labels[None, :]).astype(jnp.int32) * parents[None, :], axis=1, dtype=jnp.int32))
    itself = labels[None, :] == labels[:, None]
    ancestry = itself | (labels[None, :] == parents[:, None]) | (labels[None, :] == up_two[:, None])
    member = (segments[:, None] == labels[None, :]).astype(jnp.int32)
    tree_rows = segments.shape[0]
    lengths = lax.optimization_barrier(jnp.sum(member, axis=0, dtype=jnp.int32))
    row_index = jnp.arange(tree_rows, dtype=jnp.int32)
    first_row = lax.optimization_barrier(jnp.min(jnp.where(member > 0, row_index[:, None], tree_rows), axis=0))
    ancestor_rows = lax.optimization_barrier(jnp.sum(jnp.where(ancestry & jnp.logical_not(itself), lengths[None, :], 0), axis=1, dtype=jnp.int32))
    position = row_index + lax.optimization_barrier(jnp.sum(member * (ancestor_rows - first_row)[None, :], axis=1, dtype=jnp.int32))
    reachable = ancestry[segments.astype(jnp.int32)]
    return (position, reachable)

def route_table(routes):
    blocks = TOKEN_TOTAL // TOK_DEV
    flat_routes = routes.reshape(blocks, TOK_DEV * TOP)
    expert_hits = (flat_routes[:, :, None] == jnp.arange(EXPERTS, dtype=jnp.int32)[None, None, :]).astype(jnp.int32)
    places = lax.optimization_barrier(jnp.sum((jnp.cumsum(expert_hits, axis=1, dtype=jnp.int32) - 1) * expert_hits, axis=2, dtype=jnp.int32))
    sources = jnp.arange(blocks * TOK_DEV * TOP, dtype=jnp.int32).reshape(blocks, TOK_DEV * TOP)
    block_ids = jnp.broadcast_to(jnp.arange(blocks, dtype=jnp.int32)[:, None], flat_routes.shape)
    route_rows = jnp.full((EXPERTS, blocks, CAP), -1, jnp.int32).at[flat_routes, block_ids, places].set(sources)
    return (route_rows.reshape(EXPERTS, blocks * CAP), flat_routes.reshape(-1), (block_ids * CAP + places).reshape(-1))

def tree_attention_apply(query_tree, key_tree, value_tree, allowed):

    def one_head(pieces):
        query_one, key_one, value_one = pieces
        scores = reduced_precision_backward(jnp.einsum('trh,kh->trk', query_one, key_one, precision=EXACT_PRECISION) * HEAD_SIZE ** (-0.5))
        scores = jnp.where(allowed[:, None, :], scores, -1e+30)
        shifted = jnp.exp(scores - lax.optimization_barrier(jnp.max(scores, axis=-1, keepdims=True)))
        weights = low(shifted / lax.optimization_barrier(jnp.sum(shifted, axis=-1, keepdims=True)))
        return jnp.einsum('trk,kh->trh', weights, value_one, precision=EXACT_PRECISION)
    outcome = lax.map(jax.checkpoint(one_head), (query_tree.transpose(1, 0, 2, 3), key_tree.transpose(1, 0, 2), value_tree.transpose(1, 0, 2)))
    return outcome.transpose(1, 0, 2, 3)

def reference(tokens, out_cotangent, first_gain, query_weight, key_value_matrix, output_weight, second_gain, expert_gate_up, expert_down, routes, route_gates, expert_slot, parent_segments, token_segments):
    position_list = []
    permitted_entries = []
    for which_tree_index in range(N_DP):
        tree_segments = token_segments[which_tree_index * TREE_TOKENS:(which_tree_index + 1) * TREE_TOKENS].astype(jnp.int32)
        position, reachable = tree_layout(parent_segments[which_tree_index], tree_segments)
        row_index = jnp.arange(TREE_TOKENS, dtype=jnp.int32)
        position_list.append(position)
        permitted_entries.append(reachable[:, tree_segments] & (row_index[None, :] <= row_index[:, None]))
    positions = jnp.concatenate(position_list)
    route_rows, flat_experts, slot_rows = route_table(routes)
    query_group_count = QUERY_HEADS // KEY_VALUE_HEADS
    width_group = FF // N_TENSOR

    def experts(normed_two, weight_gate_up, weight_down):
        gate_up_sorted = weight_gate_up[expert_slot]
        down_sorted = weight_down[expert_slot]

        def one_expert(pieces):
            row_table, gate_up_one, down_one = pieces
            valid = row_table >= 0
            source = jnp.where(valid, row_table // TOP, 0)
            row_data = jnp.where(valid[:, None], normed_two[source], 0.0)
            copies = reduced_precision_backward(jnp.broadcast_to(row_data[:, None, :], (row_data.shape[0], N_TENSOR, MODEL_DIMENSION)))
            hidden = reduced_precision_backward(jnp.einsum('rgd,dgf->rgf', copies, gate_up_one.reshape(MODEL_DIMENSION, N_TENSOR, 2 * width_group), precision=EXACT_PRECISION))
            gate_part, up_part = split_pairs(hidden, PAIR)
            activation = low(swiglu(gate_part, up_part))
            expert_part = reduced_precision_backward(low(jnp.einsum('rgf,gfd->rgd', activation, down_one.reshape(N_TENSOR, width_group, MODEL_DIMENSION), precision=EXACT_PRECISION)))
            return lax.optimization_barrier(jnp.sum(expert_part, axis=1))
        outputs = lax.map(jax.checkpoint(one_expert), (route_rows, gate_up_sorted, down_sorted))
        picked = outputs[flat_experts, slot_rows].reshape(TOKEN_TOTAL, TOP, MODEL_DIMENSION)
        return jnp.einsum('tk,tkd->td', route_gates, picked, precision=EXACT_PRECISION)

    def forward(inputs, gain_one, weight_query, paired_weights, weight_out, gain_two, weight_gate_up, weight_down):
        first_normalized = low(normalize(inputs, gain_one))
        query_raw = reduced_precision_backward(jnp.dot(first_normalized, weight_query, precision=EXACT_PRECISION))
        unrotated_key_value = reduced_precision_backward(jnp.dot(first_normalized, paired_weights, precision=EXACT_PRECISION)).reshape(TOKEN_TOTAL, KEY_VALUE_HEADS, 2, HEAD_SIZE)
        query_vectors = low(rotate(query_raw.reshape(TOKEN_TOTAL, QUERY_HEADS, HEAD_SIZE), positions))
        key_matrix_rows = low(rotate(unrotated_key_value[:, :, 0], positions))
        value_matrix_rows = low(unrotated_key_value[:, :, 1])
        context_vectors = []
        for which_tree_index in range(N_DP):
            reduced_precision = which_tree_index * TREE_TOKENS
            higher_precision = reduced_precision + TREE_TOKENS
            context_vectors.append(tree_attention_apply(query_vectors[reduced_precision:higher_precision].reshape(TREE_TOKENS, KEY_VALUE_HEADS, query_group_count, HEAD_SIZE), key_matrix_rows[reduced_precision:higher_precision], value_matrix_rows[reduced_precision:higher_precision], permitted_entries[which_tree_index]))
        context = jnp.concatenate(context_vectors, axis=0).reshape(TOKEN_TOTAL, QUERY_HEADS * HEAD_SIZE)
        context = reduced_precision_backward(low(context))
        attention = reduced_precision_backward(jnp.dot(context, weight_out, precision=EXACT_PRECISION))
        hidden_state = inputs + attention
        normed_two = low(normalize(hidden_state, gain_two))
        return hidden_state + experts(normed_two, weight_gate_up, weight_down)
    floats = (tokens.astype(jnp.float32), first_gain.astype(jnp.float32), query_weight.astype(jnp.float32), key_value_matrix.astype(jnp.float32), output_weight.astype(jnp.float32), second_gain.astype(jnp.float32), expert_gate_up.astype(jnp.float32), expert_down.astype(jnp.float32))
    primal, pullback = jax.vjp(forward, *floats)
    gradients = pullback(out_cotangent.astype(jnp.float32))
    return (primal.astype(jnp.bfloat16), gradients[0].astype(jnp.bfloat16), gradients[1], gradients[2], gradients[3], gradients[4], gradients[5], gradients[6], gradients[7])
```

```python
import functools
from functools import partial

import jax
import jax.numpy as jnp
from jax import lax
from jax.experimental import pallas as pl
from jax.experimental.pallas import tpu as pltpu
from jax.sharding import PartitionSpec as P

HEAD_SIZE = 64
PAIR = 64
BF = jnp.bfloat16
F32 = jnp.float32


EPS = 1e-05


def normalize(values, gain_vector):
    inverse_rms = lax.rsqrt(jnp.mean(values * values, axis=-1, keepdims=True) + EPS)
    return values * inverse_rms * gain_vector


def rotate(values, position):
    half_width = values.shape[-1] // 2
    frequency = jnp.power(10000.0, -jnp.arange(half_width, dtype=jnp.float32) / half_width)
    angles = position.astype(jnp.float32)[:, None] * frequency[None, :]
    cosine = jnp.cos(angles)[:, None, :]
    sine_part = jnp.sin(angles)[:, None, :]
    first_half = values[..., :half_width]
    second_half = values[..., half_width:]
    return jnp.concatenate(
        [
            first_half * cosine - second_half * sine_part,
            second_half * cosine + first_half * sine_part,
        ],
        axis=-1,
    )


def tree_layout(parents, segments):
    labels = jnp.arange(parents.shape[0], dtype=jnp.int32)
    up_two = jnp.sum(
        (parents[:, None] == labels[None, :]).astype(jnp.int32) * parents[None, :],
        axis=1,
        dtype=jnp.int32,
    )
    itself = labels[None, :] == labels[:, None]
    ancestry = itself | (labels[None, :] == parents[:, None]) | (labels[None, :] == up_two[:, None])
    member = (segments[:, None] == labels[None, :]).astype(jnp.int32)
    tree_rows = segments.shape[0]
    lengths = jnp.sum(member, axis=0, dtype=jnp.int32)
    row_index = jnp.arange(tree_rows, dtype=jnp.int32)
    first_row = jnp.min(jnp.where(member > 0, row_index[:, None], tree_rows), axis=0)
    ancestor_rows = jnp.sum(
        jnp.where(ancestry & jnp.logical_not(itself), lengths[None, :], 0), axis=1, dtype=jnp.int32
    )
    position = row_index + jnp.sum(
        member * (ancestor_rows - first_row)[None, :], axis=1, dtype=jnp.int32
    )
    reachable = jnp.dot(member, ancestry.astype(jnp.int32))
    return (position, reachable, member)


def dot_nn(a,b): return lax.dot_general(a,b,(((1,),(0,)),((),())),preferred_element_type=F32)
def dot_nt(a,b): return lax.dot_general(a,b,(((1,),(1,)),((),())),preferred_element_type=F32)
def dot_tn(a,b): return lax.dot_general(a,b,(((0,),(0,)),((),())),preferred_element_type=F32)

def split_columns(w):
    low = lax.broadcasted_iota(jnp.int32, w.shape[:1] + (128,), 1) < PAIR
    gates, ups = [], []
    for i in range(w.shape[1] // 256):
        a = w[:, 256 * i : 256 * i + 128]
        b = w[:, 256 * i + 128 : 256 * i + 256]
        gates.append(jnp.where(low, a, pltpu.roll(b, PAIR, 1)))
        ups.append(jnp.where(low, pltpu.roll(a, PAIR, 1), b))
    return gates, ups

def moe_main_kernel(x_ref, c_ref, g_ref, w1_ref, w2_ref, ga_ref, hg_ref, dx_ref, acc_ref):
    step = pl.program_id(0)
    per = w1_ref.shape[0]
    units = w2_ref.shape[1]
    gates, ups = [], []
    for e in range(per):
        g, u = split_columns(w1_ref[e])
        gates += g
        ups += u
    w1 = jnp.concatenate(gates + ups, axis=1)
    w2 = w2_ref[...].reshape(per * units, w2_ref.shape[2])
    hidden = dot_nn(x_ref[...], w1)
    pull = dot_nt(c_ref[...], w2)
    lane = lax.broadcasted_iota(jnp.int32, g_ref.shape, 1)
    route = jnp.concatenate(
        [
            jnp.broadcast_to(
                jnp.sum(jnp.where(lane == step * per + e, g_ref[...], 0.0), axis=1, keepdims=True),
                (g_ref.shape[0], units),
            )
            for e in range(per)
        ],
        axis=1,
    )
    gate = hidden[:, : per * units]
    up = hidden[:, per * units :]
    sig = 1.0 / (1.0 + jnp.exp(-gate))
    silu = gate * sig
    pull = pull * route
    ga_ref[...] = (silu * up * route).astype(BF)
    hg = jnp.concatenate([pull * up * (sig * (1.0 + gate - silu)), pull * silu], axis=1).astype(BF)
    hg_ref[...] = hg
    part = dot_nt(hg, w1)

    @pl.when(step == 0)
    def _():
        acc_ref[...] = part

    @pl.when(step > 0)
    def _():
        acc_ref[...] += part

    @pl.when(step == pl.num_programs(0) - 1)
    def _():
        dx_ref[...] = acc_ref[...].astype(BF)

def moe_main(x, c, g, w1, w2):
    rows, width = x.shape
    experts, _, columns = w1.shape
    units = columns // 2
    per = 2
    whole = lambda i: (0, 0)
    return pl.pallas_call(
        moe_main_kernel,
        grid=(experts // per,),
        in_specs=[
            pl.BlockSpec((rows, width), whole),
            pl.BlockSpec((rows, width), whole),
            pl.BlockSpec((rows, g.shape[1]), whole),
            pl.BlockSpec((per, width, columns), lambda i: (i, 0, 0)),
            pl.BlockSpec((per, units, width), lambda i: (i, 0, 0)),
        ],
        out_specs=[
            pl.BlockSpec((rows, per * units), lambda i: (0, i)),
            pl.BlockSpec((rows, per * columns), lambda i: (0, i)),
            pl.BlockSpec((rows, width), whole),
        ],
        out_shape=[
            jax.ShapeDtypeStruct((rows, experts * units), BF),
            jax.ShapeDtypeStruct((rows, experts * columns), BF),
            jax.ShapeDtypeStruct((rows, width), BF),
        ],
        scratch_shapes=[pltpu.VMEM((rows, width), F32)],
        compiler_params=pltpu.CompilerParams(vmem_limit_bytes=56 << 20),
        cost_estimate=pl.CostEstimate(flops=2*rows*width*experts*columns*5//2, bytes_accessed=20<<20, transcendentals=0),
        name="experts_main",
    )(x, c, g, w1, w2)

def join_columns(gate, up):
    low = lax.broadcasted_iota(jnp.int32, gate.shape[:1] + (128,), 1) < PAIR
    out = []
    for i in range(gate.shape[1] // 128):
        g = gate[:, 128 * i : 128 * i + 128]
        u = up[:, 128 * i : 128 * i + 128]
        out.append(jnp.where(low, g, pltpu.roll(u, PAIR, 1)))
        out.append(jnp.where(low, pltpu.roll(g, PAIR, 1), u))
    return jnp.concatenate(out, axis=1)

def weight_grads_kernel(n, *refs):
    xs, cs, hgs, gas = refs[:n], refs[n : 2 * n], refs[2 * n : 3 * n], refs[3 * n : 4 * n]
    w1_ref, w2_ref, xt_ref = refs[4 * n :]
    step = pl.program_id(0)
    per, width, columns = w1_ref.shape
    units = columns // 2
    rows = xs[0].shape[0]

    @pl.when(step == 0)
    def _():
        for k in range(n):
            xt_ref[k] = xs[k][...].T

    up = down = None
    for k in range(n):
        a = dot_nn(xt_ref[k], hgs[k][...])
        b = dot_tn(gas[k][...], cs[k][...])
        up = a if up is None else up + a
        down = b if down is None else down + b
    for e in range(per):
        w1_ref[e] = join_columns(
            up[:, units * e : units * e + units], up[:, per * units + units * e : per * units + units * e + units]
        ).astype(w1_ref.dtype)
        w2_ref[e] = down[units * e : units * e + units].astype(w2_ref.dtype)

def moe_weight_grads(xs, cs, hgs, gas):
    n = len(xs)
    rows, width = xs[0].shape
    columns = 256
    units = 128
    per = 2
    experts = gas[0].shape[1] // units
    whole = lambda i: (0, 0)
    return pl.pallas_call(
        functools.partial(weight_grads_kernel, n),
        grid=(experts // per,),
        in_specs=[pl.BlockSpec((rows, width), whole, pipeline_mode=pl.Buffered(1))] * (2 * n)
        + [pl.BlockSpec((rows, per * columns), lambda i: (0, i))] * n
        + [pl.BlockSpec((rows, per * units), lambda i: (0, i))] * n,
        out_specs=[
            pl.BlockSpec((per, width, columns), lambda i: (i, 0, 0)),
            pl.BlockSpec((per, units, width), lambda i: (i, 0, 0)),
        ],
        out_shape=[
            jax.ShapeDtypeStruct((experts, width, columns), BF),
            jax.ShapeDtypeStruct((experts, units, width), BF),
        ],
        scratch_shapes=[pltpu.VMEM((n, width, rows), BF)],
        compiler_params=pltpu.CompilerParams(vmem_limit_bytes=60 << 20),
        name="experts_weights",
    )(*xs, *cs, *hgs, *gas)


def shift(values, axis, places):
    size = lax.axis_size(axis)
    return lax.ppermute(values, axis, [(i, (i + places) % size) for i in range(size)])


def swap(values, axis, bit):
    return lax.ppermute(values, axis, [(i, i ^ bit) for i in range(lax.axis_size(axis))])


def tensor_order(size):
    order = [0]
    for bit in reversed(tensor_bits(size)):
        order = order + [o ^ bit for o in order]
    return order


def tensor_bits(size):
    return [1 << b for b in range(size.bit_length() - 1)]


def gather_tensor(block):
    for bit in reversed(tensor_bits(lax.axis_size("tensor"))):
        block = jnp.concatenate([block, swap(block, "tensor", bit)], axis=0)
    return block


def reduce_tensor(blocks):
    for bit in tensor_bits(lax.axis_size("tensor")):
        half = blocks.shape[0] // 2
        received = swap(blocks[half:], "tensor", bit)
        blocks = (blocks[:half].astype(F32) + received.astype(F32)).astype(BF)
    return blocks


def to_relative(rows, order, index):
    parts = rows.reshape((len(order), rows.shape[0] // len(order)) + rows.shape[1:])
    picks = [lax.dynamic_index_in_dim(parts, index ^ o, 0, keepdims=False) for o in order]
    return jnp.concatenate(picks, axis=0)


def from_relative(rows, order, index):
    return to_relative_inverse(rows, order, index)


def to_relative_inverse(rows, order, index):
    size = len(order)
    parts = rows.reshape((size, rows.shape[0] // size) + rows.shape[1:])
    places = [order.index(o) for o in range(size)]
    picks = []
    for absolute in range(size):
        where = jnp.asarray(places, jnp.int32)[index ^ absolute]
        picks.append(lax.dynamic_index_in_dim(parts, where, 0, keepdims=False))
    return jnp.concatenate(picks, axis=0)


def attention_probs(query_vectors, all_keys, allowed, score_scale):
    scores = (
        jnp.einsum("tgrh,kgh->tgrk", query_vectors, all_keys, preferred_element_type=jnp.float32)
        * score_scale
    )
    return jnp.where(allowed[:, None, None, :], scores, -1e30)


def shards(
    tokens,
    out_cotangent,
    first_gain,
    query_weight,
    key_value_matrix,
    output_weight,
    second_gain,
    expert_gate_up,
    expert_down,
    routes,
    route_gates,
    expert_slot,
    parent_segments,
    token_segments,
):
    row_count = tokens.shape[0]
    model_width = tokens.shape[1]
    tree_rows = token_segments.shape[0]
    query_heads = query_weight.shape[1] // HEAD_SIZE
    value_heads = key_value_matrix.shape[1] // (2 * HEAD_SIZE)
    query_group_count = query_heads // value_heads
    local_experts = expert_gate_up.shape[0]
    all_experts = expert_slot.shape[0]
    devices = lax.axis_size("expert")
    tensor_size = lax.axis_size("tensor")
    tensor_index = lax.axis_index("tensor")
    order = tensor_order(tensor_size)
    part = row_count // tensor_size
    first_part = tensor_index * part
    cotangent_part = lax.dynamic_slice_in_dim(out_cotangent, first_part, part, 0)
    cotangents = [
        gather_tensor(shift(cotangent_part, "expert", k) if k else cotangent_part)
        for k in range(devices)
    ]
    slots = jnp.arange(all_experts, dtype=jnp.int32)
    slot_of = jnp.sum(
        jnp.where(routes[:, :, None] == slots[None, None, :], expert_slot[None, None, :], 0),
        axis=2,
    )
    dense = jnp.sum(
        jnp.where(slot_of[:, :, None] == slots[None, None, :], route_gates[:, :, None], 0.0), axis=1
    )
    dense = to_relative(dense, order, tensor_index)
    expert_index = lax.axis_index("expert")
    gates = []
    for k in range(devices):
        owner = (expert_index + k) % devices
        mine = lax.dynamic_slice_in_dim(dense, owner * local_experts, local_experts, 1)
        gates.append(shift(mine, "expert", k) if k else mine)
    score_scale = HEAD_SIZE ** (-0.5)
    position, reachable, member = tree_layout(parent_segments[0], token_segments)
    start_row = lax.axis_index("expert") * row_count
    own_position = lax.dynamic_slice_in_dim(position, start_row, row_count, 0)
    own_reach = lax.dynamic_slice_in_dim(reachable, start_row, row_count, 0)
    key_index = jnp.arange(tree_rows, dtype=jnp.int32)
    query_index = start_row + jnp.arange(row_count, dtype=jnp.int32)
    allowed = (jnp.dot(own_reach, member.T) > 0) & (key_index[None, :] <= query_index[:, None])
    inputs = tokens.astype(jnp.float32)
    first_float = first_gain.astype(jnp.float32)
    second_float = second_gain.astype(jnp.float32)
    first_normalized = normalize(inputs, first_float).astype(jnp.bfloat16)
    query_raw = jnp.dot(first_normalized, query_weight, preferred_element_type=jnp.float32).reshape(
        row_count, query_heads, HEAD_SIZE
    )
    unrotated_key_value = jnp.dot(
        first_normalized, key_value_matrix, preferred_element_type=jnp.float32
    ).reshape(row_count, value_heads, 2, HEAD_SIZE)
    query_vectors = (
        rotate(query_raw, own_position)
        .astype(jnp.bfloat16)
        .reshape(row_count, value_heads, query_group_count, HEAD_SIZE)
    )
    key_matrix_rows = rotate(unrotated_key_value[:, :, 0], own_position)
    key_value = (
        jnp.stack([key_matrix_rows, unrotated_key_value[:, :, 1]], axis=2)
        .astype(jnp.bfloat16)
        .reshape(row_count, value_heads * 2 * HEAD_SIZE)
    )
    gathered = lax.all_gather(key_value, "expert", axis=0, tiled=True).reshape(
        tree_rows, value_heads, 2, HEAD_SIZE
    )
    all_keys = gathered[:, :, 0]
    all_values = gathered[:, :, 1]
    scores = attention_probs(query_vectors, all_keys, allowed, score_scale)
    top_score = jnp.max(scores, axis=-1, keepdims=True)
    shifted = jnp.exp(scores - top_score)
    row_total = jnp.sum(shifted, axis=-1, keepdims=True)
    log_total = top_score + jnp.log(row_total)
    weights = (shifted / row_total).astype(jnp.bfloat16)
    context = (
        jnp.einsum("tgrk,kgh->tgrh", weights, all_values, preferred_element_type=jnp.float32)
        .astype(jnp.bfloat16)
        .reshape(row_count, query_heads * HEAD_SIZE)
    )
    partial_attention = jnp.dot(context, output_weight, preferred_element_type=F32).astype(BF)
    attention = reduce_tensor(to_relative(partial_attention, order, tensor_index)).astype(F32)
    inputs_part = lax.dynamic_slice_in_dim(tokens, first_part, part, 0).astype(F32)
    hidden_state = inputs_part + attention
    normed_two = normalize(hidden_state, second_float).astype(BF)
    normed = [
        gather_tensor(shift(normed_two, "expert", k) if k else normed_two) for k in range(devices)
    ]
    gate_up, down, added = expert_gate_up, expert_down, 0
    if gate_up.shape[2] == 2 * PAIR:
        gate_up = jnp.pad(gate_up, ((0, 0), (0, 0), (0, 2 * PAIR)))
        down = jnp.pad(down, ((0, 0), (0, PAIR), (0, 0)))
    if local_experts % 2:
        gate_up = jnp.pad(gate_up, ((0, 1), (0, 0), (0, 0)))
        down = jnp.pad(down, ((0, 1), (0, 0), (0, 0)))
    mains = [None] * devices
    back = None
    for k in list(range(1, devices)) + [0]:
        mains[k] = moe_main(normed[k], cotangents[k], gates[k], gate_up, down)
        summed = reduce_tensor(mains[k][2])
        summed = (shift(summed, "expert", devices - k) if k else summed).astype(F32)
        back = summed if back is None else back + summed
    normed_two_grad = back
    gate_up_grad, down_grad = moe_weight_grads(
        normed, cotangents, [m[1] for m in mains], [m[0] for m in mains]
    )
    gate_up_grad = gate_up_grad[:local_experts, :, : expert_gate_up.shape[2]]
    down_grad = down_grad[:local_experts, : expert_down.shape[1]]
    flat_down = down.reshape(-1, model_width)
    mixture = None
    for k in list(range(1, devices)) + [0]:
        mixed = jnp.dot(mains[k][0], flat_down, preferred_element_type=F32).astype(BF)
        summed = reduce_tensor(mixed)
        summed = (shift(summed, "expert", devices - k) if k else summed).astype(F32)
        mixture = summed if mixture is None else mixture + summed
    layer_part = (hidden_state + mixture).astype(BF)
    layer_output = from_relative(gather_tensor(layer_part), order, tensor_index)
    _, norm_two_pull = jax.vjp(normalize, hidden_state, second_float)
    hidden_norm_grad, second_gain_grad = norm_two_pull(normed_two_grad)
    residual_grad = cotangent_part.astype(F32) + hidden_norm_grad
    branch_grad = from_relative(gather_tensor(residual_grad.astype(BF)), order, tensor_index)
    output_grad = jnp.einsum("tc,td->cd", context, branch_grad, preferred_element_type=jnp.float32)
    context_grad = (
        jnp.dot(branch_grad, output_weight.T, preferred_element_type=jnp.float32)
        .astype(jnp.bfloat16)
        .reshape(row_count, value_heads, query_group_count, HEAD_SIZE)
    )
    scores = attention_probs(query_vectors, all_keys, allowed, score_scale)
    probabilities = jnp.exp(scores - log_total)
    weights = probabilities.astype(jnp.bfloat16)
    prob_grad = jnp.einsum(
        "tgrh,kgh->tgrk", context_grad, all_values, preferred_element_type=jnp.float32
    )
    row_dot = jnp.sum(probabilities * prob_grad, axis=-1, keepdims=True)
    score_grad = (probabilities * (prob_grad - row_dot)).astype(jnp.bfloat16)
    query_grad = (
        jnp.einsum("tgrk,kgh->tgrh", score_grad, all_keys, preferred_element_type=jnp.float32)
        * score_scale
    )
    key_grad = (
        jnp.einsum("tgrk,tgrh->kgh", score_grad, query_vectors, preferred_element_type=jnp.float32)
        * score_scale
    )
    value_grad = jnp.einsum(
        "tgrk,tgrh->kgh", weights, context_grad, preferred_element_type=jnp.float32
    )
    pair_grad_all = jnp.stack([key_grad, value_grad], axis=2).reshape(
        tree_rows, value_heads * 2 * HEAD_SIZE
    )
    pair_grad = (
        lax.psum_scatter(
            pair_grad_all.astype(jnp.bfloat16), "expert", scatter_dimension=0, tiled=True
        )
        .astype(jnp.float32)
        .reshape(row_count, value_heads, 2, HEAD_SIZE)
    )
    _, rotate_query_pull = jax.vjp(partial(rotate, position=own_position), query_raw)
    query_raw_grad = rotate_query_pull(query_grad.reshape(row_count, query_heads, HEAD_SIZE))[0]
    _, rotate_key_pull = jax.vjp(
        partial(rotate, position=own_position), unrotated_key_value[:, :, 0]
    )
    key_raw_grad = rotate_key_pull(pair_grad[:, :, 0])[0]
    query_low = query_raw_grad.astype(jnp.bfloat16).reshape(row_count, query_heads * HEAD_SIZE)
    pair_low = (
        jnp.stack([key_raw_grad, pair_grad[:, :, 1]], axis=2)
        .astype(jnp.bfloat16)
        .reshape(row_count, value_heads * 2 * HEAD_SIZE)
    )
    query_weight_grad = jnp.einsum(
        "td,tc->dc", first_normalized, query_low, preferred_element_type=jnp.float32
    )
    pair_weight_grad = jnp.einsum(
        "td,tc->dc", first_normalized, pair_low, preferred_element_type=jnp.float32
    )
    local_input_grad = jnp.dot(
        query_low, query_weight.T, preferred_element_type=jnp.float32
    ) + jnp.dot(pair_low, key_value_matrix.T, preferred_element_type=jnp.float32)
    normed_one_grad = reduce_tensor(
        to_relative(local_input_grad.astype(BF), order, tensor_index)
    ).astype(F32)
    _, norm_one_pull = jax.vjp(normalize, inputs_part, first_float)
    input_norm_grad, first_gain_grad = norm_one_pull(normed_one_grad)
    input_part = (residual_grad + input_norm_grad).astype(BF)
    input_gradient = from_relative(gather_tensor(input_part), order, tensor_index)
    gains = jnp.stack([first_gain_grad, second_gain_grad])
    for axis in ("tensor", "dp", "expert"):
        for bit in tensor_bits(lax.axis_size(axis)):
            gains = gains + swap(gains, axis, bit)
    shared = [
        lax.psum(grad.astype(BF), ("dp", "expert")).astype(F32)
        for grad in (query_weight_grad, pair_weight_grad, output_grad)
    ]
    gate_up_total = gate_up_grad.astype(F32) + shift(gate_up_grad, "dp", 1).astype(F32)
    down_total = down_grad.astype(F32) + shift(down_grad, "dp", 1).astype(F32)
    shared = [gains[0]] + shared + [gains[1]]
    return (
        layer_output,
        input_gradient,
        shared[0],
        shared[1],
        shared[2],
        shared[3],
        shared[4],
        gate_up_total,
        down_total,
    )


def solution(mesh):
    in_specs = (
        P(("dp", "expert"), None),
        P(("dp", "expert"), None),
        P(),
        P(None, "tensor"),
        P(None, "tensor"),
        P("tensor", None),
        P(),
        P("expert", None, "tensor"),
        P("expert", "tensor", None),
        P(("dp", "expert"), None),
        P(("dp", "expert"), None),
        P(),
        P("dp", None),
        P("dp"),
    )
    out_specs = (
        P(("dp", "expert"), None),
        P(("dp", "expert"), None),
        P(),
        P(None, "tensor"),
        P(None, "tensor"),
        P("tensor", None),
        P(),
        P("expert", None, "tensor"),
        P("expert", "tensor", None),
    )
    return jax.shard_map(shards, mesh=mesh, in_specs=in_specs, out_specs=out_specs, check_vma=False)
```

```python
import functools
import math

import jax
import jax.numpy as jnp
import numpy as np
from jax import lax
from jax.experimental import pallas as pl
from jax.experimental.pallas import tpu as pltpu
from jax.sharding import PartitionSpec as P

HEAD_SIZE = 64
PAIR = 64
BF = jnp.bfloat16
F32 = jnp.float32
EPS = 1e-05


def normalize(values, gain_vector):
    inverse_rms = lax.rsqrt(jnp.mean(values * values, axis=-1, keepdims=True) + EPS)
    return values * inverse_rms * gain_vector


SMEM = pl.BlockSpec(memory_space=pltpu.SMEM)
VMEM = pl.BlockSpec(memory_space=pltpu.VMEM)
CHEAP = pl.CostEstimate(flops=1000, bytes_accessed=1000, transcendentals=0)


def roomy(mebibytes):
    return pltpu.CompilerParams(vmem_limit_bytes=mebibytes << 20)


def dot_nn(a, b):
    return lax.dot_general(a, b, (((1,), (0,)), ((), ())), preferred_element_type=F32)


def dot_nt(a, b):
    return lax.dot_general(a, b, (((1,), (1,)), ((), ())), preferred_element_type=F32)


def dot_tn(a, b):
    return lax.dot_general(a, b, (((0,), (0,)), ((), ())), preferred_element_type=F32)


def split_columns(w):
    low = lax.broadcasted_iota(jnp.int32, w.shape[:1] + (128,), 1) < PAIR
    gates, ups = [], []
    for i in range(w.shape[1] // 256):
        a = w[:, 256 * i : 256 * i + 128]
        b = w[:, 256 * i + 128 : 256 * i + 256]
        gates.append(jnp.where(low, a, pltpu.roll(b, PAIR, 1)))
        ups.append(jnp.where(low, pltpu.roll(a, PAIR, 1), b))
    return gates, ups


def join_columns(gate, up):
    low = lax.broadcasted_iota(jnp.int32, gate.shape[:1] + (128,), 1) < PAIR
    out = []
    for i in range(gate.shape[1] // 128):
        g = gate[:, 128 * i : 128 * i + 128]
        u = up[:, 128 * i : 128 * i + 128]
        out.append(jnp.where(low, g, pltpu.roll(u, PAIR, 1)))
        out.append(jnp.where(low, pltpu.roll(g, PAIR, 1), u))
    return jnp.concatenate(out, axis=1)


def expert_step(
    first, all_experts, x_ref, c_ref, g_ref, w1_ref, w2_ref, ga_ref, hg_ref, acc_ref
):
    per, width, columns = w1_ref.shape
    units = columns // 2
    gates, ups = [], []
    for e in range(per):
        g, u = split_columns(w1_ref[e])
        gates += g
        ups += u
    w1 = jnp.concatenate(gates + ups, axis=1)
    w2 = w2_ref[...].reshape(per * units, width)
    half = x_ref.shape[0] // 2
    parts = [slice(0, half), slice(half, 2 * half)]
    fronts = [(dot_nn(x_ref[s], w1), dot_nt(c_ref[s], w2)) for s in parts]
    for s, (hidden, pull) in zip(parts, fronts):
        weights = g_ref[s].astype(F32)
        lane = lax.broadcasted_iota(jnp.int32, weights.shape, 1)
        route = []
        for e in range(per):
            mine = (lane == first + e) | (lane == first + e + all_experts)
            weight = jnp.sum(jnp.where(mine, weights, 0.0), axis=1, keepdims=True)
            route.append(jnp.broadcast_to(weight, (half, units)))
        route = jnp.concatenate(route, axis=1)
        gate = hidden[:, : per * units]
        up = hidden[:, per * units :]
        sig = 1.0 / (1.0 + jnp.exp(-gate))
        silu = gate * sig
        pull = pull * route
        activation = (silu * up * route).astype(BF)
        ga_ref[s] = activation
        gate_grad = (pull * up * (sig * (1.0 + gate - silu))).astype(BF)
        up_grad = (pull * silu).astype(BF)
        hg_ref[s] = join_columns(gate_grad, up_grad)
        if acc_ref is not None:
            acc_ref[s] += dot_nt(jnp.concatenate([gate_grad, up_grad], axis=1), w1)


def main_kernel(
    all_experts, place_ref, x_ref, c_ref, g_ref, w1_ref, w2_ref, ga_ref, hg_ref, kept_ref,
    sent_ref, acc_ref,
):
    step = pl.program_id(0)

    @pl.when(step == 0)
    def _():
        acc_ref[...] = jnp.zeros_like(acc_ref)

    first = place_ref[1] + step * w1_ref.shape[0]
    expert_step(first, all_experts, x_ref, c_ref, g_ref, w1_ref, w2_ref, ga_ref, hg_ref, acc_ref)

    @pl.when(step == pl.num_programs(0) - 1)
    def _():
        write_halves(acc_ref, place_ref[2], kept_ref, sent_ref)


def other_kernel(all_experts, place_ref, x_ref, c_ref, g_ref, w1_ref, w2_ref, ga_ref, hg_ref):
    first = place_ref[1] + place_ref[3] * w1_ref.shape[0]
    expert_step(first, all_experts, x_ref, c_ref, g_ref, w1_ref, w2_ref, ga_ref, hg_ref, None)


class Rows:
    def __init__(self, array, index=None):
        self.array, self.index = array, index

    def spec(self, rows, width, column=0):
        index = self.index
        return pl.BlockSpec(
            (rows, width),
            lambda i, place: (place[0] if index is None else index, column),
            pipeline_mode=pl.Buffered(1),
        )


def experts_main(place, x, c, g, g_column, w1, w2, rows, all_experts, part):
    experts, width, columns = w1.shape
    units = columns // 2
    per = 2
    half = (rows // (2 * part), part, width)
    return pl.pallas_call(
        functools.partial(main_kernel, all_experts),
        grid_spec=pltpu.PrefetchScalarGridSpec(
            num_scalar_prefetch=1,
            grid=(experts // per,),
            in_specs=[
                x.spec(rows, width),
                c.spec(rows, width),
                g.spec(rows, 128, g_column),
                pl.BlockSpec((per, width, columns), lambda i, p: (i, 0, 0)),
                pl.BlockSpec((per, units, width), lambda i, p: (i, 0, 0)),
            ],
            out_specs=[
                pl.BlockSpec((rows, per * units), lambda i, p: (0, i)),
                pl.BlockSpec((rows, per * columns), lambda i, p: (0, i)),
                pl.BlockSpec(half, lambda i, p: (0, 0, 0)),
                pl.BlockSpec(half, lambda i, p: (0, 0, 0)),
            ],
            scratch_shapes=[pltpu.VMEM((rows, width), F32)],
        ),
        out_shape=[
            jax.ShapeDtypeStruct((rows, experts * units), BF),
            jax.ShapeDtypeStruct((rows, experts * columns), BF),
            jax.ShapeDtypeStruct(half, BF),
            jax.ShapeDtypeStruct(half, BF),
        ],
        compiler_params=roomy(48),
        cost_estimate=CHEAP,
        name="experts_main",
    )(place, x.array, c.array, g.array, w1, w2)


def experts_other(place, x, c, w1, w2, rows, all_experts):
    experts, width, columns = w1.shape
    units = columns // 2
    per = experts // 2
    groups = x.shape[0] // rows
    once = pl.Buffered(1)
    other = lambda i, p: (1 - p[3]) * groups + i
    return pl.pallas_call(
        functools.partial(other_kernel, all_experts),
        grid_spec=pltpu.PrefetchScalarGridSpec(
            num_scalar_prefetch=1,
            grid=(groups,),
            in_specs=[
                pl.BlockSpec((rows, width), lambda i, p: (i, 0)),
                pl.BlockSpec((rows, width), lambda i, p: (other(i, p), 0)),
                pl.BlockSpec((rows, 128), lambda i, p: (other(i, p), width // 128)),
                pl.BlockSpec((per, width, columns), lambda i, p: (p[3], 0, 0), pipeline_mode=once),
                pl.BlockSpec((per, units, width), lambda i, p: (p[3], 0, 0), pipeline_mode=once),
            ],
            out_specs=[
                pl.BlockSpec((rows, per * units), lambda i, p: (i, 0)),
                pl.BlockSpec((rows, per * columns), lambda i, p: (i, 0)),
            ],
        ),
        out_shape=[
            jax.ShapeDtypeStruct((groups * rows, per * units), BF),
            jax.ShapeDtypeStruct((groups * rows, per * columns), BF),
        ],
        compiler_params=roomy(60),
        cost_estimate=CHEAP,
        name="experts_other",
    )(place, x, c, c, w1, w2)


def weights_kernel(groups, count, half, first, place_ref, *refs):
    m = len(groups)
    xs, c_hbm, hgs, gas = refs[:m], refs[m], refs[m + 1 : 2 * m + 1], refs[2 * m + 1 : 3 * m + 1]
    out_ref, x_ref, c_ref, hg_ref, ga_ref, up_ref, down_ref, sems = refs[3 * m + 1 :]
    _, rows, width = x_ref.shape
    columns = out_ref.shape[2]
    units = columns // 2
    tree, zone = place_ref[3], place_ref[4]
    for k, (x_index, h_index, shift_by, total) in enumerate(groups):
        if shift_by is None:
            group = (1 - tree) * total + h_index
            expert = first
        else:
            group = tree * total + lax.rem(zone + total - shift_by, total)
            expert = tree * half + first
        c_rows = pl.ds(pl.multiple_of(group * rows, 32), rows)
        h_rows = pl.ds(h_index * rows, rows)
        for i, copy in enumerate(
            (
                (xs[k].at[pl.ds(x_index * rows, rows)], x_ref),
                (hgs[k].at[h_rows, pl.ds(pl.multiple_of(expert * columns, 128), count * columns)], hg_ref),
                (c_hbm.at[c_rows, pl.ds(0, width)], c_ref),
                (gas[k].at[h_rows, pl.ds(pl.multiple_of(expert * units, 128), count * units)], ga_ref),
            )
        ):
            pltpu.make_async_copy(copy[0], copy[1].at[k], sems.at[i, k]).start()
    up_ref[...] = jnp.zeros_like(up_ref)
    down_ref[...] = jnp.zeros_like(down_ref)

    def body(k, carry):
        for i, ref in enumerate((x_ref, hg_ref)):
            pltpu.make_async_copy(ref.at[k], ref.at[k], sems.at[i, k]).wait()
        up_ref[...] += dot_tn(x_ref[k], hg_ref[k])
        for i, ref in enumerate((c_ref, ga_ref)):
            pltpu.make_async_copy(ref.at[k], ref.at[k], sems.at[2 + i, k]).wait()
        down_ref[...] += dot_tn(ga_ref[k], c_ref[k])
        return carry

    lax.fori_loop(0, m, body, 0)
    for e in range(count):
        out_ref[e, :width] = up_ref[:, columns * e : columns * (e + 1)].astype(BF)
        for t in range(width // columns):
            out_ref[e, width + units * t : width + units * (t + 1)] = down_ref[
                units * e : units * (e + 1), columns * t : columns * t + columns
            ].astype(BF)


def experts_weights(place, groups, c, first, count, half, rows):
    width = groups[0][0].shape[1]
    units = 2 * PAIR
    columns = 2 * units
    m = len(groups)
    hbm = pl.BlockSpec(memory_space=pl.ANY)
    return pl.pallas_call(
        functools.partial(weights_kernel, [g[3:] for g in groups], count, half, first),
        in_specs=[SMEM] + [hbm] * (3 * m + 1),
        out_specs=VMEM,
        out_shape=jax.ShapeDtypeStruct((count, width + width // 2, columns), BF),
        scratch_shapes=[
            pltpu.VMEM((m, rows, width), BF),
            pltpu.VMEM((m, rows, width), BF),
            pltpu.VMEM((m, rows, count * columns), BF),
            pltpu.VMEM((m, rows, count * units), BF),
            pltpu.VMEM((width, count * columns), F32),
            pltpu.VMEM((count * units, width), F32),
            pltpu.SemaphoreType.DMA((4, m)),
        ],
        compiler_params=roomy(60),
        cost_estimate=CHEAP,
        name="experts_weights",
    )(place, *[g[0] for g in groups], c, *[g[1] for g in groups], *[g[2] for g in groups])


def finish_kernel(source, *refs):
    o1_ref, o2_ref = refs[-2:]
    width, columns = o1_ref.shape[1:]
    units = o2_ref.shape[1]
    stored = source.shape[2]
    total = source[0].astype(F32)
    o1_ref[0] = total[:width, :columns]
    for t in range(width // stored):
        rows = total[width + stored // 2 * t : width + stored // 2 * (t + 1)]
        o2_ref[0, :, stored * t : stored * (t + 1)] = rows[:units]


def finish_weights(grads, before, first, half, up_shape, down_shape):
    extra = [] if before is None else list(before)
    count = grads.shape[0] // 2
    if 2 * half > up_shape[0] and first + count == half:
        steps = 2 * count - 1
    else:
        steps = 2 * count
    place = lambda i: (i // count) * half + first + i % count
    return pl.pallas_call(
        finish_kernel,
        grid=(steps,),
        in_specs=[pl.BlockSpec((1,) + grads.shape[1:], lambda i: (i, 0, 0))]
        + [pl.BlockSpec(memory_space=pl.ANY)] * len(extra),
        out_specs=[
            pl.BlockSpec((1,) + up_shape[1:], lambda i: (place(i), 0, 0)),
            pl.BlockSpec((1,) + down_shape[1:], lambda i: (place(i), 0, 0)),
        ],
        out_shape=[jax.ShapeDtypeStruct(up_shape, F32), jax.ShapeDtypeStruct(down_shape, F32)],
        input_output_aliases={1: 0, 2: 1} if extra else {},
        compiler_params=roomy(60),
        cost_estimate=CHEAP,
        name="finish_weights",
    )(grads, *extra)


def write_halves(total_ref, core, kept_ref, sent_ref):
    part = kept_ref.shape[1]
    for n in range(kept_ref.shape[0]):
        pair = 2 * n * part
        own = core * part
        if part % 8:
            low = total_ref[pair : pair + part]
            high = total_ref[pair + part : pair + 2 * part]
            kept_ref[n] = jnp.where(own == 0, low, high).astype(BF)
            sent_ref[n] = jnp.where(own == 0, high, low).astype(BF)
        else:
            other = pl.multiple_of(pair + part - own, 8)
            own = pl.multiple_of(pair + own, 8)
            kept_ref[n] = total_ref[pl.ds(own, part)].astype(BF)
            sent_ref[n] = total_ref[pl.ds(other, part)].astype(BF)


def block_info_kernel_part(zone, seg_ref, par_ref, info_ref, block):
    blocks = info_ref.shape[0]
    slots = info_ref.shape[1] - 1
    total = seg_ref.shape[0] // block
    counts = []
    for a in range(blocks):
        mine = zone * blocks + a
        own = seg_ref[mine * block]
        above = par_ref[0, own]
        top = par_ref[0, above]
        count = jnp.int32(0)
        for c in range(total - 1):
            other = seg_ref[c * block]
            seen = (c < mine) & ((other == own) | (other == above) | (other == top))
            info_ref[a, jnp.minimum(count, slots - 1)] = (zone - c // blocks) * blocks + c % blocks
            count = count + seen.astype(jnp.int32)
        info_ref[a, slots] = count
        counts.append(count)
    return counts


def rope_angles(count, cos_ref, sin_ref, far_cos_ref, far_sin_ref):
    far_cos = far_cos_ref[pl.ds(count, 1)]
    far_sin = far_sin_ref[pl.ds(count, 1)]
    return (
        cos_ref[...] * far_cos - sin_ref[...] * far_sin,
        sin_ref[...] * far_cos + cos_ref[...] * far_sin,
    )


def turn(values, cosine, sine):
    lane = lax.broadcasted_iota(jnp.int32, values.shape, 1)
    crossed = jnp.where(
        lane % HEAD_SIZE < HEAD_SIZE // 2, -pltpu.roll(values, 96, 1), pltpu.roll(values, 32, 1)
    )
    return values * cosine + crossed * sine


def rope_tables(block, slots):
    frequency = 10000.0 ** (-np.arange(HEAD_SIZE // 2) / (HEAD_SIZE // 2))
    frequency = np.tile(frequency, 4)[None]
    near = np.arange(block)[:, None] * frequency
    far = np.arange(slots)[:, None] * block * frequency
    return [jnp.asarray(f(a), F32) for a in (near, far) for f in (np.cos, np.sin)]


def key_value_kernel(
    zone_ref, seg_ref, par_ref, x_ref, gain_ref, w_ref, c_ref, s_ref, fc_ref, fs_ref,
    normed_ref, kv_ref, info_ref,
):
    block = c_ref.shape[0]
    counts = block_info_kernel_part(zone_ref[0], seg_ref, par_ref, info_ref, block)
    x = x_ref[...].astype(F32)
    inverse = lax.rsqrt(jnp.mean(x * x, axis=-1, keepdims=True) + EPS)
    normed = (x * inverse * gain_ref[...].astype(F32)).astype(BF)
    normed_ref[...] = normed
    raw = dot_nn(normed, w_ref[...])
    low = lax.broadcasted_iota(jnp.int32, (block, 128), 1) < HEAD_SIZE
    for a, count in enumerate(counts):
        cosine, sine = rope_angles(count, c_ref, s_ref, fc_ref, fs_ref)
        rows = slice(a * block, (a + 1) * block)
        for t in range(raw.shape[1] // 128):
            tile = raw[rows, 128 * t : 128 * t + 128]
            kv_ref[rows, 128 * t : 128 * t + 128] = jnp.where(
                low, turn(tile, cosine, sine), tile
            ).astype(BF)


def query_kernel(info_ref, normed_ref, w_ref, c_ref, s_ref, fc_ref, fs_ref, q_ref):
    block = c_ref.shape[0]
    blocks = info_ref.shape[0]
    slots = info_ref.shape[1] - 1
    raw = dot_nn(normed_ref[...], w_ref[...])
    for a in range(blocks):
        cosine, sine = rope_angles(info_ref[a, slots], c_ref, s_ref, fc_ref, fs_ref)
        rows = slice(a * block, (a + 1) * block)
        for t in range(raw.shape[1] // 128):
            tile = raw[rows, 128 * t : 128 * t + 128]
            q_ref[rows, 128 * t : 128 * t + 128] = (
                turn(tile, cosine, sine).astype(BF).astype(F32) * HEAD_SIZE**-0.5
            ).astype(BF)


def head_low(tiles, head):
    tile = tiles[:, 128 * (head // 2) : 128 * (head // 2) + 128]
    low = lax.broadcasted_iota(jnp.int32, tile.shape, 1) < HEAD_SIZE
    if head % 2:
        tile = pltpu.roll(tile, HEAD_SIZE, 1)
    return jnp.where(low, tile, jnp.zeros_like(tile))


def head_high(tiles, head):
    tile = tiles[:, 128 * (head // 2) : 128 * (head // 2) + 128]
    low = lax.broadcasted_iota(jnp.int32, tile.shape, 1) < HEAD_SIZE
    if head % 2 == 0:
        tile = pltpu.roll(tile, HEAD_SIZE, 1)
    return jnp.where(low, jnp.zeros_like(tile), tile)


def collect(info_ref, kv_ref, seen_ref, step, block, group):
    slots = info_ref.shape[1] - 1
    count = info_ref[step, slots]
    columns = slice(128 * group, 128 * group + 128)
    for m in range(slots - 1):
        source = jnp.where(m < count, info_ref[step, m], 0)
        seen_ref[m * block : (m + 1) * block] = kv_ref[
            pl.ds(pl.multiple_of(source * block, 32), block), columns
        ]
    seen_ref[(slots - 1) * block : slots * block] = kv_ref[
        pl.ds(pl.multiple_of(step * block, 32), block), columns
    ]
    if seen_ref.shape[0] > slots * block:
        seen_ref[slots * block :] = jnp.zeros_like(seen_ref[slots * block :])
    return seen_ref[...]


def seen_mask(info_ref, step, block, width):
    slots = info_ref.shape[1] - 1
    column = lax.broadcasted_iota(jnp.int32, (block, width), 1)
    row = lax.broadcasted_iota(jnp.int32, (block, width), 0)
    before = (slots - 1) * block
    return (column < info_ref[step, slots] * block) | (
        (column >= before) & (column - before <= row)
    )


def attention_kernel(
    groups, heads, info_ref, place_ref, q_ref, kv_ref, wo_ref, ctx_ref, lse_ref, kept_ref, sent_ref,
    seen_ref, out_ref,
):
    step = pl.program_id(0)
    block = q_ref.shape[0]
    per = heads // groups
    mask = seen_mask(info_ref, step, block, seen_ref.shape[0])
    mask = jnp.concatenate([mask] * per, axis=0)
    queries = q_ref[...]
    lane = lax.broadcasted_iota(jnp.int32, lse_ref.shape, 1)
    totals = jnp.zeros(lse_ref.shape, F32)
    found = []
    for g in range(groups):
        seen = collect(info_ref, kv_ref, seen_ref, step, block, g)
        packed = jnp.concatenate([head_low(queries, g * per + r) for r in range(per)], axis=0)
        scores = jnp.where(mask, dot_nt(packed, seen), -1e30)
        top = jnp.max(scores, axis=1, keepdims=True)
        shifted = jnp.exp(scores - top)
        total = jnp.sum(shifted, axis=1, keepdims=True)
        result = dot_nn(shifted.astype(BF), seen) / total
        log_total = top + jnp.log(total)
        for r in range(per):
            rows = slice(r * block, (r + 1) * block)
            found.append(result[rows])
            totals = jnp.where(lane == g * per + r, log_total[rows], totals)
    lse_ref[...] = totals
    low = lax.broadcasted_iota(jnp.int32, (block, 128), 1) < HEAD_SIZE
    tiles = []
    for t in range(ctx_ref.shape[1] // 128):
        left = pltpu.roll(found[2 * t], HEAD_SIZE, 1)
        right = found[2 * t + 1] if 2 * t + 1 < heads else jnp.zeros_like(left)
        tiles.append(jnp.where(low, left, right).astype(BF))
    context = jnp.concatenate(tiles, axis=1)
    ctx_ref[...] = context
    out_ref[pl.ds(pl.multiple_of(step * block, 32), block)] = dot_nn(context, wo_ref[...])

    @pl.when(step == pl.num_programs(0) - 1)
    def _():
        write_halves(out_ref, place_ref[2], kept_ref, sent_ref)


def attention_back_kernel(
    groups, heads, info_ref, place_ref, q_ref, kv_ref, lse_ref, g_ref, ctx_ref, n_ref, wo_ref,
    c_ref, s_ref, fc_ref, fs_ref, dq_ref, dkv_ref, kept_ref, sent_ref, seen_ref, acc_ref,
    out_grad_ref, q_grad_ref,
):
    step = pl.program_id(0)
    block = q_ref.shape[0]
    slots = info_ref.shape[1] - 1
    per = heads // groups

    @pl.when(step == 0)
    def _():
        acc_ref[...] = jnp.zeros_like(acc_ref)
        out_grad_ref[...] = jnp.zeros_like(out_grad_ref)
        q_grad_ref[...] = jnp.zeros_like(q_grad_ref)

    mask = seen_mask(info_ref, step, block, seen_ref.shape[0])
    mask = jnp.concatenate([mask] * per, axis=0)
    queries = q_ref[...]
    out_grad_ref[...] += dot_tn(ctx_ref[...], g_ref[...])
    pulled = dot_nt(g_ref[...], wo_ref[...]).astype(BF)
    lane = lax.broadcasted_iota(jnp.int32, lse_ref.shape, 1)
    count = info_ref[step, slots]
    found = []
    for g in range(groups):
        seen = collect(info_ref, kv_ref, seen_ref, step, block, g)
        packed = jnp.concatenate([head_low(queries, g * per + r) for r in range(per)], axis=0)
        grads = jnp.concatenate([head_high(pulled, g * per + r) for r in range(per)], axis=0)
        log_total = jnp.concatenate(
            [
                jnp.sum(jnp.where(lane == g * per + r, lse_ref[...], 0.0), axis=1, keepdims=True)
                for r in range(per)
            ],
            axis=0,
        )
        scores = jnp.where(mask, dot_nt(packed, seen), -1e30)
        probabilities = jnp.exp(scores - log_total)
        prob_grad = dot_nt(grads, seen)
        row_dot = jnp.sum(probabilities * prob_grad, axis=1, keepdims=True)
        score_grad = (probabilities * (prob_grad - row_dot)).astype(BF)
        query_grad = dot_nn(score_grad, seen)
        pair_grad = (dot_tn(packed, score_grad) + dot_tn(grads, probabilities.astype(BF))).T
        for r in range(per):
            found.append(query_grad[r * block : (r + 1) * block])
        columns = slice(128 * g, 128 * g + 128)
        for m in range(slots - 1):

            @pl.when(m < count)
            def _():
                rows = pl.ds(pl.multiple_of(info_ref[step, m] * block, 32), block)
                acc_ref[rows, columns] += pair_grad[m * block : (m + 1) * block]

        rows = pl.ds(pl.multiple_of(step * block, 32), block)
        acc_ref[rows, columns] += pair_grad[(slots - 1) * block : slots * block]
    cosine, sine = rope_angles(count, c_ref, s_ref, fc_ref, fs_ref)
    low = lax.broadcasted_iota(jnp.int32, (block, 128), 1) < HEAD_SIZE
    for t in range(dq_ref.shape[1] // 128):
        left = found[2 * t]
        right = (
            pltpu.roll(found[2 * t + 1], HEAD_SIZE, 1)
            if 2 * t + 1 < heads
            else jnp.zeros_like(left)
        )
        tile = jnp.where(low, left, right) * HEAD_SIZE**-0.5
        dq_ref[:, 128 * t : 128 * t + 128] = turn(tile, cosine, -sine).astype(BF)

    q_grad_ref[...] += dot_tn(dq_ref[...], n_ref[...])

    @pl.when(step == pl.num_programs(0) - 1)
    def _():
        dkv_ref[...] = acc_ref[...].astype(BF)
        rows = kept_ref.shape[0]

        @pl.when(place_ref[3] == 0)
        def _():
            kept_ref[...] = out_grad_ref[:rows].astype(BF)
            sent_ref[...] = q_grad_ref[:rows].astype(BF)

        @pl.when(place_ref[3] != 0)
        def _():
            kept_ref[...] = q_grad_ref[:rows].astype(BF)
            sent_ref[...] = out_grad_ref[:rows].astype(BF)


def project_back_kernel(info_ref, place_ref, *refs):
    *pieces, n_ref, dq_ref, wq_ref, wkv_ref, c_ref, s_ref, fc_ref, fs_ref = refs[:-7]
    kept_ref, sent_ref, kept_kv_ref, sent_kv_ref, low_ref, back_ref, grad_ref = refs[-7:]
    block = c_ref.shape[0]
    blocks = info_ref.shape[0]
    slots = info_ref.shape[1] - 1
    total = pieces[0][...].astype(F32)
    for piece in pieces[1:]:
        total = total + piece[...].astype(F32)
    low = lax.broadcasted_iota(jnp.int32, (block, 128), 1) < HEAD_SIZE
    for a in range(blocks):
        cosine, sine = rope_angles(info_ref[a, slots], c_ref, s_ref, fc_ref, fs_ref)
        rows = slice(a * block, (a + 1) * block)
        for t in range(total.shape[1] // 128):
            tile = total[rows, 128 * t : 128 * t + 128]
            low_ref[rows, 128 * t : 128 * t + 128] = jnp.where(
                low, turn(tile, cosine, -sine), tile
            ).astype(BF)
    back_ref[...] = dot_nt(dq_ref[...], wq_ref[...]) + dot_nt(low_ref[...], wkv_ref[...])
    write_halves(back_ref, place_ref[2], kept_ref, sent_ref)
    grad_ref[...] = dot_tn(low_ref[...], n_ref[...])
    share = kept_kv_ref.shape[0]
    own = pl.multiple_of(place_ref[3] * share, 8)
    other = pl.multiple_of(share - own, 8)
    kept_kv_ref[...] = grad_ref[pl.ds(own, share)].astype(BF)
    sent_kv_ref[...] = grad_ref[pl.ds(other, share)].astype(BF)


def project_key_value(zone, segments, parents, tokens, gain, weight, tables, blocks, slots):
    rows, width = tokens.shape
    whole = lambda i: (0, 0)
    operands = (tokens, gain[None], weight, *tables)
    return pl.pallas_call(
        key_value_kernel,
        grid=(1,),
        in_specs=[SMEM] * 3 + [pl.BlockSpec(o.shape, whole) for o in operands],
        out_specs=[
            pl.BlockSpec((rows, width), whole),
            pl.BlockSpec((rows, weight.shape[1]), whole),
            SMEM,
        ],
        out_shape=[
            jax.ShapeDtypeStruct((rows, width), BF),
            jax.ShapeDtypeStruct((rows, weight.shape[1]), BF),
            jax.ShapeDtypeStruct((blocks, slots + 1), jnp.int32),
        ],
        compiler_params=roomy(32),
        cost_estimate=CHEAP,
        name="project_key_value",
    )(zone, segments, parents, *operands)


def project_query(info, normed, weight, tables):
    return pl.pallas_call(
        query_kernel,
        in_specs=[SMEM] + [VMEM] * 6,
        out_specs=VMEM,
        out_shape=jax.ShapeDtypeStruct((normed.shape[0], weight.shape[1]), BF),
        compiler_params=roomy(32),
        cost_estimate=CHEAP,
        name="project_query",
    )(info, normed, weight, *tables)


def lanes_up(size):
    return -(-size // 128) * 128


def attention_forward(info, place, queries, key_value, output_weight, heads, part):
    rows, columns = queries.shape
    blocks, slots = info.shape[0], info.shape[1] - 1
    block = rows // blocks
    groups = key_value.shape[1] // 128
    width = output_weight.shape[1]
    by_block = lambda i, *_: (i, 0)
    whole = lambda i, *_: (0, 0)
    half = (rows // (2 * part), part, width)
    return pl.pallas_call(
        functools.partial(attention_kernel, groups, heads),
        grid_spec=pltpu.PrefetchScalarGridSpec(
            num_scalar_prefetch=2,
            grid=(blocks,),
            in_specs=[
                pl.BlockSpec((block, columns), by_block),
                pl.BlockSpec(key_value.shape, whole),
                pl.BlockSpec(output_weight.shape, whole),
            ],
            out_specs=[
                pl.BlockSpec((block, columns), by_block),
                pl.BlockSpec((block, 128), by_block),
                pl.BlockSpec(half, lambda i, *_: (0, 0, 0)),
                pl.BlockSpec(half, lambda i, *_: (0, 0, 0)),
            ],
            scratch_shapes=[
                pltpu.VMEM((lanes_up(slots * block), 128), BF),
                pltpu.VMEM((rows, width), F32),
            ],
        ),
        out_shape=[
            jax.ShapeDtypeStruct((rows, columns), BF),
            jax.ShapeDtypeStruct((rows, 128), F32),
            jax.ShapeDtypeStruct(half, BF),
            jax.ShapeDtypeStruct(half, BF),
        ],
        compiler_params=roomy(48),
        cost_estimate=CHEAP,
        name="attention_forward",
    )(info, place, queries, key_value, output_weight)


def attention_backward(
    info, place, queries, key_value, log_totals, branch_grad, context, normed, output_weight,
    tables, heads,
):
    rows, columns = queries.shape
    blocks, slots = info.shape[0], info.shape[1] - 1
    block = rows // blocks
    groups = key_value.shape[1] // 128
    width = output_weight.shape[1]
    by_block = lambda i, *_: (i, 0)
    whole = lambda i, *_: (0, 0)
    share = (heads * HEAD_SIZE, width)
    return pl.pallas_call(
        functools.partial(attention_back_kernel, groups, heads),
        grid_spec=pltpu.PrefetchScalarGridSpec(
            num_scalar_prefetch=2,
            grid=(blocks,),
            in_specs=[
                pl.BlockSpec((block, columns), by_block),
                pl.BlockSpec(key_value.shape, whole),
                pl.BlockSpec((block, 128), by_block),
                pl.BlockSpec((block, width), by_block),
                pl.BlockSpec((block, columns), by_block),
                pl.BlockSpec((block, width), by_block),
                pl.BlockSpec(output_weight.shape, whole),
            ]
            + [pl.BlockSpec(t.shape, whole) for t in tables],
            out_specs=[
                pl.BlockSpec((block, columns), by_block),
                pl.BlockSpec(key_value.shape, whole),
                pl.BlockSpec(share, whole),
                pl.BlockSpec(share, whole),
            ],
            scratch_shapes=[
                pltpu.VMEM((lanes_up(slots * block), 128), BF),
                pltpu.VMEM(key_value.shape, F32),
                pltpu.VMEM((columns, width), F32),
                pltpu.VMEM((columns, width), F32),
            ],
        ),
        out_shape=[
            jax.ShapeDtypeStruct((rows, columns), BF),
            jax.ShapeDtypeStruct(key_value.shape, BF),
            jax.ShapeDtypeStruct(share, BF),
            jax.ShapeDtypeStruct(share, BF),
        ],
        compiler_params=roomy(56),
        cost_estimate=CHEAP,
        name="attention_backward",
    )(info, place, queries, key_value, log_totals, branch_grad, context, normed, output_weight, *tables)


def project_backward(info, place, pieces, normed, query_low, query_weight, pair_weight, tables, part):
    rows, width = normed.shape
    columns = pair_weight.shape[1]
    half = (rows // (2 * part), part, width)
    share = (columns // 2, width)
    return pl.pallas_call(
        project_back_kernel,
        in_specs=[SMEM] * 2 + [VMEM] * (len(pieces) + 8),
        out_specs=[VMEM] * 4,
        out_shape=[jax.ShapeDtypeStruct(shape, BF) for shape in (half, half, share, share)],
        scratch_shapes=[
            pltpu.VMEM((rows, columns), BF),
            pltpu.VMEM((rows, width), F32),
            pltpu.VMEM((columns, width), F32),
        ],
        compiler_params=roomy(48),
        cost_estimate=CHEAP,
        name="project_backward",
    )(info, place, *pieces, normed, query_low, query_weight, pair_weight, *tables)


def shift(values, axis, places):
    size = lax.axis_size(axis)
    return lax.ppermute(values, axis, [(i, (i + places) % size) for i in range(size)])


def slide(values, axis, places):
    size = lax.axis_size(axis)
    return lax.ppermute(
        values, axis, [(i, i + places) for i in range(size) if 0 <= i + places < size]
    )


def swap(values, axis, bit):
    return lax.ppermute(values, axis, [(i, i ^ bit) for i in range(lax.axis_size(axis))])


def bits_of(size):
    return [1 << b for b in range(size.bit_length() - 1)]


def hold(values, *others):
    return lax.optimization_barrier((values,) + others)[0]


def halves(held, bit):
    pairs = held.reshape(held.shape[:1] + (held.shape[1] // 2, 2) + held.shape[2:])
    mine = jnp.where((lax.axis_index("tensor") & bit) != 0, 1, 0)
    return (
        lax.dynamic_index_in_dim(pairs, mine, 2, keepdims=False),
        lax.dynamic_index_in_dim(pairs, 1 - mine, 2, keepdims=False),
    )


class Line:
    def __init__(self):
        self.last = None

    def mark(self, value):
        self.last = value
        return value

    def take(self, values):
        if isinstance(values, list):
            return list(lax.optimization_barrier((*values, self.last))[:-1])
        return hold(values, self.last)

    def after(self, values, others):
        return hold(values, others)


class Gathering:
    def __init__(self, line, pieces):
        self.held = line.mark(jnp.stack(pieces)[:, None])
        self.bits = bits_of(lax.axis_size("tensor"))[::-1]
        self.send(line)

    def send(self, line):
        if self.bits:
            self.coming = swap(self.held, "tensor", self.bits[0])

    def step(self, line):
        other = line.take(self.coming)
        mine = (lax.axis_index("tensor") & self.bits[0]) != 0
        held = jnp.where(
            mine, jnp.stack([other, self.held], axis=2), jnp.stack([self.held, other], axis=2)
        )
        self.held = line.mark(held.reshape((held.shape[0], -1) + held.shape[3:]))
        self.bits = self.bits[1:]
        self.send(line)

    def rows(self):
        return self.held.reshape(-1, self.held.shape[-1])


class Summing:
    def __init__(self, line, rows=None, split=None):
        size = lax.axis_size("tensor")
        self.bits = bits_of(size)
        if split is None:
            self.held = rows.reshape((rows.shape[0], size, -1) + rows.shape[2:])
            self.send(line)
        else:
            self.kept, sent = split
            self.coming = swap(line.take(sent), "tensor", self.bits[0])

    def send(self, line):
        if self.bits:
            self.kept, sent = halves(self.held, self.bits[0])
            self.coming = swap(line.mark(sent), "tensor", self.bits[0])

    def step(self, line):
        coming = line.take(self.coming)
        self.held = line.mark((self.kept.astype(F32) + coming.astype(F32)).astype(BF))
        self.bits = self.bits[1:]
        self.send(line)


class Mixing:
    def __init__(self, line, groups, part):
        self.bits = bits_of(lax.axis_size("tensor"))
        both = [halves(g.reshape(1, -1, part, g.shape[1]), self.bits[0]) for g in groups]
        self.kept = jnp.concatenate([b[0] for b in both], axis=0)
        sent = line.mark(jnp.concatenate([b[1] for b in both], axis=0))
        self.coming = swap(sent, "tensor", self.bits[0])

    def step(self, line):
        coming = line.take(self.coming)
        self.held = line.mark((self.kept.astype(F32) + coming.astype(F32)).astype(BF))
        self.bits = self.bits[1:]
        if self.bits:
            self.kept, sent = halves(self.held, self.bits[0])
            self.coming = swap(line.mark(sent), "tensor", self.bits[0])

    def homes(self, line):
        groups = line.take(self.held[:, 0])
        size = groups.shape[0]
        return [groups[0]] + [shift(groups[k], "expert", size - k) for k in range(1, size)]


class Exchange:
    def __init__(self, line, half, up_shape, down_shape):
        self.line, self.half, self.shapes = line, half, (up_shape, down_shape)
        self.waiting, self.flying, self.landed, self.totals = [], None, [], None
        self.done = 0

    def add(self, grads):
        self.waiting.append(self.line.mark(grads))
        if self.flying is None:
            self.begin()

    def begin(self):
        grads = self.line.take(self.waiting.pop(0))
        self.flying = lax.all_gather(grads, "dp", axis=0, tiled=True)

    def land(self):
        if self.flying is not None:
            self.landed.append(self.line.mark(self.line.take(self.flying)))
            self.flying = None
            if self.waiting:
                self.begin()

    def settle(self):
        while self.landed:
            grads = self.line.take(self.landed.pop(0))
            self.totals = finish_weights(grads, self.totals, self.done, self.half, *self.shapes)
            self.line.mark(self.totals[1])
            self.done += grads.shape[0] // 2


class AllSum:
    def __init__(self, line, kept, sent):
        self.kept = kept
        self.size = lax.axis_size("expert")
        self.coming = swap(line.take(sent), "dp", 1)
        self.stage = 0

    def spread(self, blocks):
        return lax.all_to_all(blocks, "expert", split_axis=0, concat_axis=0)

    def step(self, line):
        coming = line.take(self.coming)
        if self.stage == 0:
            both = line.mark((self.kept.astype(F32) + coming.astype(F32)).astype(BF))
            self.coming = self.spread(both.reshape((self.size, -1) + both.shape[1:]))
        elif self.stage == 1:
            total = coming[0].astype(F32)
            for k in range(1, self.size):
                total = total + coming[k].astype(F32)
            own = line.mark(jnp.broadcast_to(total.astype(BF)[None], coming.shape))
            self.coming = self.spread(own)
        elif self.stage == 2:
            self.own = line.mark(coming.reshape(self.kept.shape))
            self.coming = swap(self.own, "dp", 1)
        else:
            first = lax.axis_index("dp") == 0
            self.shares = (
                jnp.where(first, self.own, coming).astype(F32),
                jnp.where(first, coming, self.own).astype(F32),
            )
            line.mark(self.shares[0])
        self.stage += 1


class SmallSum:
    def __init__(self, line, values):
        self.values = values
        self.coming = swap(line.take(values), "dp", 1)
        self.stage = 0

    def step(self, line):
        coming = line.take(self.coming)
        if self.stage == 0:
            both = self.values + coming
            size = lax.axis_size("expert")
            own = line.mark(jnp.broadcast_to(both[None], (size,) + both.shape))
            self.coming = lax.all_to_all(own, "expert", split_axis=0, concat_axis=0)
        else:
            self.values = line.mark(jnp.sum(coming, axis=0))
        self.stage += 1


def shards(
    tokens,
    out_cotangent,
    first_gain,
    query_weight,
    key_value_matrix,
    output_weight,
    second_gain,
    expert_gate_up,
    expert_down,
    routes,
    route_gates,
    expert_slot,
    parent_segments,
    token_segments,
):
    row_count, width = tokens.shape
    tree_rows = token_segments.shape[0]
    query_columns = query_weight.shape[1]
    heads = query_columns // HEAD_SIZE
    local_experts = expert_gate_up.shape[0]
    all_experts = expert_slot.shape[0]
    devices = lax.axis_size("expert")
    zone = lax.axis_index("expert")
    tensor_bits = bits_of(lax.axis_size("tensor"))
    core = lax.axis_index("tensor") % 2
    part = row_count // lax.axis_size("tensor")
    first_part = lax.axis_index("tensor") * part
    leaf = tree_rows // 12
    block = math.gcd(leaf, row_count)
    blocks = row_count // block
    slots = 7 * leaf // block
    tables = rope_tables(block, slots)
    if query_columns % 128:
        query_weight = jnp.pad(query_weight, ((0, 0), (0, HEAD_SIZE)))
        output_weight = jnp.pad(output_weight, ((0, HEAD_SIZE), (0, 0)))

    normed_one, key_value, info = project_key_value(
        zone[None].astype(jnp.int32), token_segments, parent_segments, tokens, first_gain,
        key_value_matrix, tables, blocks, slots,
    )
    key_values = [key_value] + [slide(key_value, "expert", k) for k in range(1, devices)]
    queries = project_query(info, normed_one, query_weight, tables)
    experts_range = jnp.arange(all_experts, dtype=jnp.int32)[None, None, :]
    routed = jnp.sum(
        jnp.where(routes[:, :, None] == experts_range, expert_slot[None, None, :], 0), axis=2
    )
    dense = jnp.sum(
        jnp.where(routed[:, :, None] == experts_range, route_gates[:, :, None], 0.0), axis=1
    )
    dense_high = lax.reduce_precision(dense, 8, 7)
    own_gates = jnp.concatenate(
        [
            dense_high.astype(BF),
            (dense - dense_high).astype(BF),
            jnp.zeros((row_count, 128 - 2 * all_experts), BF),
        ],
        axis=1,
    )
    cotangent_part = lax.dynamic_slice_in_dim(out_cotangent, first_part, part, 0)
    gates_part = lax.dynamic_slice_in_dim(own_gates, first_part, part, 0)
    all_cotangents = lax.all_gather(
        jnp.concatenate([cotangent_part, gates_part], axis=1),
        ("dp", "expert", "tensor"),
        axis=0,
        tiled=True,
    )
    line = Line()
    line.mark(queries)
    key_values = line.mark(jnp.concatenate(line.take(key_values), axis=0))
    tree = lax.axis_index("dp")
    places = [
        jnp.stack(
            [tree * devices + (zone - k) % devices, zone * local_experts, core, tree, zone]
        ).astype(jnp.int32)
        for k in range(devices)
    ]
    context, log_totals, *split = attention_forward(
        info, places[0], queries, key_values, output_weight, heads, part
    )
    line.mark(context)
    summing = Summing(line, split=[h[None] for h in split])
    while summing.bits:
        summing.step(line)
    attention = summing.held[0, 0].astype(F32)
    inputs_part = lax.dynamic_slice_in_dim(tokens, first_part, part, 0).astype(F32)
    hidden_state = inputs_part + attention
    second_float = second_gain.astype(F32)
    normed_two = line.mark(normalize(hidden_state, second_float).astype(BF))

    gate_up, down = expert_gate_up, expert_down
    if gate_up.shape[2] == 2 * PAIR:
        gate_up = jnp.pad(gate_up, ((0, 0), (0, 0), (0, 2 * PAIR)))
        down = jnp.pad(down, ((0, 0), (0, PAIR), (0, 0)))
    if local_experts % 2:
        gate_up = jnp.pad(gate_up, ((0, 1), (0, 0), (0, 0)))
        down = jnp.pad(down, ((0, 1), (0, 0), (0, 0)))
    experts = gate_up.shape[0]
    half = experts // 2
    cots = [Rows(out_cotangent, 0)] + [Rows(all_cotangents) for _ in range(1, devices)]
    gates = [(Rows(own_gates, 0), 0)] + [(Rows(all_cotangents), width // 128)] * (devices - 1)
    xs = [None] * devices
    mains = [None] * devices
    running, homes = [], []
    total = None

    def advance(total):
        while homes:
            home = line.mark(line.take(homes.pop(0))).astype(F32)
            total = home if total is None else total + home
        for k, summing in list(running):
            summing.step(line)
            if not summing.bits:
                running.remove((k, summing))
                own = line.take(summing.held[0, 0])
                homes.append(shift(own, "expert", devices - k) if k else own)
        return total

    def run_main(k, total):
        mains[k] = experts_main(
            places[k], Rows(line.take(xs[k].array), xs[k].index), cots[k], *gates[k], gate_up,
            down, row_count, all_experts, part,
        )
        line.mark(mains[k][2])
        total = advance(total)
        running.append((k, Summing(line, split=[h[None] for h in mains[k][2:]])))
        return total

    nearest = shift(normed_two, "expert", 1)
    own_rows = Gathering(line, [normed_two])
    other_part = swap(normed_two, "dp", 1)
    nearest = line.mark(line.take(nearest))
    near_rows = Gathering(line, [nearest])
    own_rows.step(line)
    others = [shift(line.take(normed_two), "expert", k) for k in range(2, devices)]
    while own_rows.bits:
        own_rows.step(line)
    xs[0] = Rows(own_rows.rows(), 0)
    total = run_main(0, total)
    other_part = line.mark(line.take(other_part))
    x_other = lax.all_gather(other_part, ("expert", "tensor"), axis=0, tiled=True)
    near_rows.step(line)
    far = []
    for k in range(2, devices, 2):
        far.append(Gathering(line, line.take(others[k - 2 : k])))
    while near_rows.bits:
        near_rows.step(line)
    xs[1] = Rows(near_rows.rows(), 0)
    total = run_main(1, total)
    for n, gathering in enumerate(far):
        while gathering.bits:
            gathering.step(line)
            total = advance(total)
        rows = gathering.rows()
        for j in range(2):
            xs[2 + 2 * n + j] = Rows(rows, j)
            total = run_main(2 + 2 * n + j, total)
    hidden_grads, activations = [k[1] for k in mains], [k[0] for k in mains]
    flat_down = down.reshape(-1, width)
    mixed = []
    while running or homes:
        if len(mixed) < devices:
            array = line.take(activations[len(mixed)])
            mixed.append(
                line.mark(jnp.dot(array, flat_down, preferred_element_type=F32).astype(BF))
            )
        total = advance(total)
    while len(mixed) < devices:
        array = line.take(activations[len(mixed)])
        mixed.append(line.mark(jnp.dot(array, flat_down, preferred_element_type=F32).astype(BF)))
    normed_two_grad = total
    _, norm_two_pull = jax.vjp(normalize, hidden_state, second_float)
    hidden_norm_grad, second_gain_grad = norm_two_pull(normed_two_grad)
    residual_grad = line.mark(cotangent_part.astype(F32) + hidden_norm_grad)

    gathering = Gathering(line, [residual_grad.astype(BF)])
    mixing = Mixing(line, line.take(mixed), part)
    ga_other, hg_other = experts_other(
        places[0], line.take(x_other), all_cotangents, gate_up, down, row_count, all_experts
    )
    line.mark(ga_other)

    def weight_grads(first, count):
        x_late = line.take(x_other)
        groups = [
            (xs[k].array, hidden_grads[k], activations[k], xs[k].index, 0, k, devices)
            for k in range(devices)
        ] + [(x_late, hg_other, ga_other, k, k, None, devices) for k in range(devices)]
        parts = [
            experts_weights(
                places[0], groups[g : g + 8], all_cotangents, first, count, half, row_count
            )
            for g in range(0, len(groups), 8)
        ]
        if len(parts) == 1:
            return parts[0]
        return sum(p.astype(F32) for p in parts).astype(BF)

    exchange = Exchange(line, half, expert_gate_up.shape, expert_down.shape)
    split_count = (half + 1) // 2
    gathering.step(line)
    mixing.step(line)
    while gathering.bits:
        gathering.step(line)
    branch_grad = line.mark(gathering.rows())
    query_low, pair_all, *split = attention_backward(
        info, places[0], queries, key_values, log_totals, line.take(branch_grad), context,
        normed_one, output_weight, tables, heads,
    )
    line.mark(query_low)
    pieces = line.take(pair_all).reshape(devices, row_count, pair_all.shape[1])
    pieces = [pieces[0]] + [slide(pieces[k], "expert", -k) for k in range(1, devices)]
    outer_sum = AllSum(line, *split)
    first_grads = line.mark(weight_grads(0, split_count))
    pieces = line.take(pieces)
    line.mark(pieces[1])
    exchange.add(first_grads)
    *split, pair_kept, pair_sent = project_backward(
        info, places[0], pieces, normed_one, query_low, query_weight, key_value_matrix, tables,
        part,
    )
    line.mark(pair_kept)
    summing = Summing(line, split=[h[None] for h in split])
    outer_sum.step(line)
    pair_sum = AllSum(line, pair_kept, pair_sent)
    summing.step(line)
    last_grads = line.mark(weight_grads(split_count, half - split_count))
    while summing.bits:
        summing.step(line)
    outer_sum.step(line)
    pair_sum.step(line)
    while mixing.bits:
        mixing.step(line)
    normed_one_grad = summing.held[0, 0].astype(F32)
    _, norm_one_pull = jax.vjp(normalize, inputs_part, first_gain.astype(F32))
    input_norm_grad, first_gain_grad = norm_one_pull(normed_one_grad)
    input_part = line.mark((residual_grad + input_norm_grad).astype(BF))
    extra = jnp.zeros((8, width), F32).at[0].set(first_gain_grad).at[1].set(second_gain_grad)
    gathering = Gathering(line, [jnp.concatenate([input_part, extra.astype(BF)], axis=0)])
    homes = mixing.homes(line)
    exchange.add(last_grads)
    gathering.step(line)
    outer_sum.step(line)
    pair_sum.step(line)
    while gathering.bits:
        gathering.step(line)
    exchange.land()
    rows = gathering.held.reshape(-1, part + 8, width)
    input_gradient = rows[:, :part].reshape(row_count, width)
    gains = SmallSum(line, jnp.sum(rows[:, part:].astype(F32), axis=0))
    mixture = homes[0].astype(F32)
    for home in homes[1:]:
        mixture = mixture + line.take(home).astype(F32)
    gathering = Gathering(line, [line.mark((hidden_state + mixture).astype(BF))])
    pair_sum.step(line)
    gains.step(line)
    outer_sum.step(line)
    gathering.step(line)
    while gathering.bits:
        gathering.step(line)
    layer_output = gathering.rows()
    pair_sum.step(line)
    exchange.settle()
    gains.step(line)
    gains = gains.values
    while exchange.flying is not None:
        exchange.land()
        exchange.settle()
    totals = exchange.totals
    return (
        layer_output,
        input_gradient,
        gains[0],
        outer_sum.shares[1].T,
        jnp.concatenate(pair_sum.shares, axis=0).T,
        outer_sum.shares[0],
        gains[1],
        *totals,
    )


def solution(mesh):
    in_specs = (
        P(("dp", "expert"), None),
        P(("dp", "expert"), None),
        P(),
        P(None, "tensor"),
        P(None, "tensor"),
        P("tensor", None),
        P(),
        P("expert", None, "tensor"),
        P("expert", "tensor", None),
        P(("dp", "expert"), None),
        P(("dp", "expert"), None),
        P(),
        P("dp", None),
        P("dp"),
    )
    out_specs = (
        P(("dp", "expert"), None),
        P(("dp", "expert"), None),
        P(),
        P(None, "tensor"),
        P(None, "tensor"),
        P("tensor", None),
        P(),
        P("expert", None, "tensor"),
        P("expert", "tensor", None),
    )
    return jax.shard_map(shards, mesh=mesh, in_specs=in_specs, out_specs=out_specs, check_vma=False)
```

```python
import functools
import math

import jax
import jax.numpy as jnp
import numpy as np
from jax import lax
from jax.experimental import pallas as pl
from jax.experimental.pallas import tpu as pltpu
from jax.sharding import PartitionSpec as P

HEAD_SIZE = 64
PAIR = 64
BF = jnp.bfloat16
F32 = jnp.float32
EPS = 1e-05


def normalize(values, gain_vector):
    inverse_rms = lax.rsqrt(jnp.mean(values * values, axis=-1, keepdims=True) + EPS)
    return values * inverse_rms * gain_vector


SMEM = pl.BlockSpec(memory_space=pltpu.SMEM)
VMEM = pl.BlockSpec(memory_space=pltpu.VMEM)
CHEAP = pl.CostEstimate(flops=1000, bytes_accessed=1000, transcendentals=0)


def roomy(mebibytes):
    return pltpu.CompilerParams(vmem_limit_bytes=mebibytes << 20)


def dot_nn(a, b):
    return lax.dot_general(a, b, (((1,), (0,)), ((), ())), preferred_element_type=F32)


def dot_nt(a, b):
    return lax.dot_general(a, b, (((1,), (1,)), ((), ())), preferred_element_type=F32)


def dot_tn(a, b):
    return lax.dot_general(a, b, (((0,), (0,)), ((), ())), preferred_element_type=F32)


def split_columns(w):
    low = lax.broadcasted_iota(jnp.int32, w.shape[:1] + (128,), 1) < PAIR
    gates, ups = [], []
    for i in range(w.shape[1] // 256):
        a = w[:, 256 * i : 256 * i + 128]
        b = w[:, 256 * i + 128 : 256 * i + 256]
        gates.append(jnp.where(low, a, pltpu.roll(b, PAIR, 1)))
        ups.append(jnp.where(low, pltpu.roll(a, PAIR, 1), b))
    return gates, ups


def join_columns(gate, up):
    low = lax.broadcasted_iota(jnp.int32, gate.shape[:1] + (128,), 1) < PAIR
    out = []
    for i in range(gate.shape[1] // 128):
        g = gate[:, 128 * i : 128 * i + 128]
        u = up[:, 128 * i : 128 * i + 128]
        out.append(jnp.where(low, g, pltpu.roll(u, PAIR, 1)))
        out.append(jnp.where(low, pltpu.roll(g, PAIR, 1), u))
    return jnp.concatenate(out, axis=1)


def expert_step(
    first, all_experts, x_ref, c_ref, g_ref, w1_ref, w2_ref, ga_ref, hg_ref, acc_ref
):
    per, width, columns = w1_ref.shape
    units = columns // 2
    gates, ups = [], []
    for e in range(per):
        g, u = split_columns(w1_ref[e])
        gates += g
        ups += u
    w1 = jnp.concatenate(gates + ups, axis=1)
    w2 = w2_ref[...].reshape(per * units, width)
    half = x_ref.shape[0] // 2
    parts = [slice(0, half), slice(half, 2 * half)]
    fronts = [(dot_nn(x_ref[s], w1), dot_nt(c_ref[s], w2)) for s in parts]
    for s, (hidden, pull) in zip(parts, fronts):
        weights = g_ref[s].astype(F32)
        lane = lax.broadcasted_iota(jnp.int32, weights.shape, 1)
        route = []
        for e in range(per):
            mine = (lane == first + e) | (lane == first + e + all_experts)
            weight = jnp.sum(jnp.where(mine, weights, 0.0), axis=1, keepdims=True)
            route.append(jnp.broadcast_to(weight, (half, units)))
        route = jnp.concatenate(route, axis=1)
        gate = hidden[:, : per * units]
        up = hidden[:, per * units :]
        sig = 1.0 / (1.0 + jnp.exp(-gate))
        silu = gate * sig
        pull = pull * route
        activation = (silu * up * route).astype(BF)
        ga_ref[s] = activation
        gate_grad = (pull * up * (sig * (1.0 + gate - silu))).astype(BF)
        up_grad = (pull * silu).astype(BF)
        hg_ref[s] = join_columns(gate_grad, up_grad)
        if acc_ref is not None:
            acc_ref[s] += dot_nt(jnp.concatenate([gate_grad, up_grad], axis=1), w1)


def main_kernel(
    all_experts, place_ref, x_ref, c_ref, g_ref, w1_ref, w2_ref, ga_ref, hg_ref, kept_ref,
    sent_ref, acc_ref,
):
    step = pl.program_id(0)

    @pl.when(step == 0)
    def _():
        acc_ref[...] = jnp.zeros_like(acc_ref)

    first = place_ref[1] + step * w1_ref.shape[0]
    expert_step(first, all_experts, x_ref, c_ref, g_ref, w1_ref, w2_ref, ga_ref, hg_ref, acc_ref)

    @pl.when(step == pl.num_programs(0) - 1)
    def _():
        write_halves(acc_ref, place_ref[2], kept_ref, sent_ref)


def other_kernel(all_experts, place_ref, x_ref, c_ref, g_ref, w1_ref, w2_ref, ga_ref, hg_ref):
    first = place_ref[1] + place_ref[3] * w1_ref.shape[0]
    expert_step(first, all_experts, x_ref, c_ref, g_ref, w1_ref, w2_ref, ga_ref, hg_ref, None)


class Rows:
    def __init__(self, array, index=None):
        self.array, self.index = array, index

    def spec(self, rows, width, column=0):
        index = self.index
        return pl.BlockSpec(
            (rows, width),
            lambda i, place: (place[0] if index is None else index, column),
            pipeline_mode=pl.Buffered(1),
        )


def experts_main(place, x, c, g, g_column, w1, w2, rows, all_experts, part):
    experts, width, columns = w1.shape
    units = columns // 2
    per = 2
    half = (rows // (2 * part), part, width)
    return pl.pallas_call(
        functools.partial(main_kernel, all_experts),
        grid_spec=pltpu.PrefetchScalarGridSpec(
            num_scalar_prefetch=1,
            grid=(experts // per,),
            in_specs=[
                x.spec(rows, width),
                c.spec(rows, width),
                g.spec(rows, 128, g_column),
                pl.BlockSpec((per, width, columns), lambda i, p: (i, 0, 0)),
                pl.BlockSpec((per, units, width), lambda i, p: (i, 0, 0)),
            ],
            out_specs=[
                pl.BlockSpec((rows, per * units), lambda i, p: (0, i)),
                pl.BlockSpec((rows, per * columns), lambda i, p: (0, i)),
                pl.BlockSpec(half, lambda i, p: (0, 0, 0)),
                pl.BlockSpec(half, lambda i, p: (0, 0, 0)),
            ],
            scratch_shapes=[pltpu.VMEM((rows, width), F32)],
        ),
        out_shape=[
            jax.ShapeDtypeStruct((rows, experts * units), BF),
            jax.ShapeDtypeStruct((rows, experts * columns), BF),
            jax.ShapeDtypeStruct(half, BF),
            jax.ShapeDtypeStruct(half, BF),
        ],
        compiler_params=roomy(48),
        cost_estimate=CHEAP,
        name="experts_main",
    )(place, x.array, c.array, g.array, w1, w2)


def experts_other(place, x, c, w1, w2, rows, all_experts):
    experts, width, columns = w1.shape
    units = columns // 2
    per = experts // 2
    groups = x.shape[0] // rows
    once = pl.Buffered(1)
    other = lambda i, p: (1 - p[3]) * groups + i
    return pl.pallas_call(
        functools.partial(other_kernel, all_experts),
        grid_spec=pltpu.PrefetchScalarGridSpec(
            num_scalar_prefetch=1,
            grid=(groups,),
            in_specs=[
                pl.BlockSpec((rows, width), lambda i, p: (i, 0)),
                pl.BlockSpec((rows, width), lambda i, p: (other(i, p), 0)),
                pl.BlockSpec((rows, 128), lambda i, p: (other(i, p), width // 128)),
                pl.BlockSpec((per, width, columns), lambda i, p: (p[3], 0, 0), pipeline_mode=once),
                pl.BlockSpec((per, units, width), lambda i, p: (p[3], 0, 0), pipeline_mode=once),
            ],
            out_specs=[
                pl.BlockSpec((rows, per * units), lambda i, p: (i, 0)),
                pl.BlockSpec((rows, per * columns), lambda i, p: (i, 0)),
            ],
        ),
        out_shape=[
            jax.ShapeDtypeStruct((groups * rows, per * units), BF),
            jax.ShapeDtypeStruct((groups * rows, per * columns), BF),
        ],
        compiler_params=roomy(60),
        cost_estimate=CHEAP,
        name="experts_other",
    )(place, x, c, c, w1, w2)


def weights_kernel(groups, count, half, first, place_ref, *refs):
    m = len(groups)
    xs, c_hbm, hgs, gas = refs[:m], refs[m], refs[m + 1 : 2 * m + 1], refs[2 * m + 1 : 3 * m + 1]
    out_ref, x_ref, c_ref, hg_ref, ga_ref, up_ref, down_ref, sems = refs[3 * m + 1 :]
    _, rows, width = x_ref.shape
    columns = out_ref.shape[2]
    units = columns // 2
    tree, zone = place_ref[3], place_ref[4]
    for k, (x_index, h_index, shift_by, total) in enumerate(groups):
        if shift_by is None:
            group = (1 - tree) * total + h_index
            expert = first
        else:
            group = tree * total + lax.rem(zone + total - shift_by, total)
            expert = tree * half + first
        c_rows = pl.ds(pl.multiple_of(group * rows, 32), rows)
        h_rows = pl.ds(h_index * rows, rows)
        for i, copy in enumerate(
            (
                (xs[k].at[pl.ds(x_index * rows, rows)], x_ref),
                (hgs[k].at[h_rows, pl.ds(pl.multiple_of(expert * columns, 128), count * columns)], hg_ref),
                (c_hbm.at[c_rows, pl.ds(0, width)], c_ref),
                (gas[k].at[h_rows, pl.ds(pl.multiple_of(expert * units, 128), count * units)], ga_ref),
            )
        ):
            pltpu.make_async_copy(copy[0], copy[1].at[k], sems.at[i, k]).start()
    up_ref[...] = jnp.zeros_like(up_ref)
    down_ref[...] = jnp.zeros_like(down_ref)

    def body(k, carry):
        for i, ref in enumerate((x_ref, hg_ref)):
            pltpu.make_async_copy(ref.at[k], ref.at[k], sems.at[i, k]).wait()
        up_ref[...] += dot_tn(x_ref[k], hg_ref[k])
        for i, ref in enumerate((c_ref, ga_ref)):
            pltpu.make_async_copy(ref.at[k], ref.at[k], sems.at[2 + i, k]).wait()
        down_ref[...] += dot_tn(ga_ref[k], c_ref[k])
        return carry

    lax.fori_loop(0, m, body, 0)
    for e in range(count):
        out_ref[e, :width] = up_ref[:, columns * e : columns * (e + 1)].astype(BF)
        for t in range(width // columns):
            out_ref[e, width + units * t : width + units * (t + 1)] = down_ref[
                units * e : units * (e + 1), columns * t : columns * t + columns
            ].astype(BF)


def experts_weights(place, groups, c, first, count, half, rows):
    width = groups[0][0].shape[1]
    units = 2 * PAIR
    columns = 2 * units
    m = len(groups)
    hbm = pl.BlockSpec(memory_space=pl.ANY)
    return pl.pallas_call(
        functools.partial(weights_kernel, [g[3:] for g in groups], count, half, first),
        in_specs=[SMEM] + [hbm] * (3 * m + 1),
        out_specs=VMEM,
        out_shape=jax.ShapeDtypeStruct((count, width + width // 2, columns), BF),
        scratch_shapes=[
            pltpu.VMEM((m, rows, width), BF),
            pltpu.VMEM((m, rows, width), BF),
            pltpu.VMEM((m, rows, count * columns), BF),
            pltpu.VMEM((m, rows, count * units), BF),
            pltpu.VMEM((width, count * columns), F32),
            pltpu.VMEM((count * units, width), F32),
            pltpu.SemaphoreType.DMA((4, m)),
        ],
        compiler_params=roomy(60),
        cost_estimate=CHEAP,
        name="experts_weights",
    )(place, *[g[0] for g in groups], c, *[g[1] for g in groups], *[g[2] for g in groups])


def finish_kernel(source, *refs):
    o1_ref, o2_ref = refs[-2:]
    width, columns = o1_ref.shape[1:]
    units = o2_ref.shape[1]
    stored = source.shape[2]
    total = source[0].astype(F32)
    o1_ref[0] = total[:width, :columns]
    for t in range(width // stored):
        rows = total[width + stored // 2 * t : width + stored // 2 * (t + 1)]
        o2_ref[0, :, stored * t : stored * (t + 1)] = rows[:units]


def finish_weights(grads, before, first, half, up_shape, down_shape):
    extra = [] if before is None else list(before)
    count = grads.shape[0] // 2
    if 2 * half > up_shape[0] and first + count == half:
        steps = 2 * count - 1
    else:
        steps = 2 * count
    place = lambda i: (i // count) * half + first + i % count
    return pl.pallas_call(
        finish_kernel,
        grid=(steps,),
        in_specs=[pl.BlockSpec((1,) + grads.shape[1:], lambda i: (i, 0, 0))]
        + [pl.BlockSpec(memory_space=pl.ANY)] * len(extra),
        out_specs=[
            pl.BlockSpec((1,) + up_shape[1:], lambda i: (place(i), 0, 0)),
            pl.BlockSpec((1,) + down_shape[1:], lambda i: (place(i), 0, 0)),
        ],
        out_shape=[jax.ShapeDtypeStruct(up_shape, F32), jax.ShapeDtypeStruct(down_shape, F32)],
        input_output_aliases={1: 0, 2: 1} if extra else {},
        compiler_params=roomy(60),
        cost_estimate=CHEAP,
        name="finish_weights",
    )(grads, *extra)


def write_halves(total_ref, core, kept_ref, sent_ref):
    part = kept_ref.shape[1]
    for n in range(kept_ref.shape[0]):
        pair = 2 * n * part
        own = core * part
        if part % 8:
            low = total_ref[pair : pair + part]
            high = total_ref[pair + part : pair + 2 * part]
            kept_ref[n] = jnp.where(own == 0, low, high).astype(BF)
            sent_ref[n] = jnp.where(own == 0, high, low).astype(BF)
        else:
            other = pl.multiple_of(pair + part - own, 8)
            own = pl.multiple_of(pair + own, 8)
            kept_ref[n] = total_ref[pl.ds(own, part)].astype(BF)
            sent_ref[n] = total_ref[pl.ds(other, part)].astype(BF)


def block_info_kernel_part(zone, seg_ref, par_ref, info_ref, block):
    blocks = info_ref.shape[0]
    slots = info_ref.shape[1] - 1
    total = seg_ref.shape[0] // block
    counts = []
    for a in range(blocks):
        mine = zone * blocks + a
        own = seg_ref[mine * block]
        above = par_ref[0, own]
        top = par_ref[0, above]
        count = jnp.int32(0)
        for c in range(total - 1):
            other = seg_ref[c * block]
            seen = (c < mine) & ((other == own) | (other == above) | (other == top))
            info_ref[a, jnp.minimum(count, slots - 1)] = (zone - c // blocks) * blocks + c % blocks
            count = count + seen.astype(jnp.int32)
        info_ref[a, slots] = count
        counts.append(count)
    return counts


def rope_angles(count, cos_ref, sin_ref, far_cos_ref, far_sin_ref):
    far_cos = far_cos_ref[pl.ds(count, 1)]
    far_sin = far_sin_ref[pl.ds(count, 1)]
    return (
        cos_ref[...] * far_cos - sin_ref[...] * far_sin,
        sin_ref[...] * far_cos + cos_ref[...] * far_sin,
    )


def turn(values, cosine, sine):
    lane = lax.broadcasted_iota(jnp.int32, values.shape, 1)
    crossed = jnp.where(
        lane % HEAD_SIZE < HEAD_SIZE // 2, -pltpu.roll(values, 96, 1), pltpu.roll(values, 32, 1)
    )
    return values * cosine + crossed * sine


def rope_tables(block, slots):
    frequency = 10000.0 ** (-np.arange(HEAD_SIZE // 2) / (HEAD_SIZE // 2))
    frequency = np.tile(frequency, 4)[None]
    near = np.arange(block)[:, None] * frequency
    far = np.arange(slots)[:, None] * block * frequency
    return [jnp.asarray(f(a), F32) for a in (near, far) for f in (np.cos, np.sin)]


def key_value_kernel(
    zone_ref, seg_ref, par_ref, x_ref, gain_ref, w_ref, c_ref, s_ref, fc_ref, fs_ref,
    normed_ref, kv_ref, info_ref,
):
    block = c_ref.shape[0]
    counts = block_info_kernel_part(zone_ref[0], seg_ref, par_ref, info_ref, block)
    x = x_ref[...].astype(F32)
    inverse = lax.rsqrt(jnp.mean(x * x, axis=-1, keepdims=True) + EPS)
    normed = (x * inverse * gain_ref[...].astype(F32)).astype(BF)
    normed_ref[...] = normed
    raw = dot_nn(normed, w_ref[...])
    low = lax.broadcasted_iota(jnp.int32, (block, 128), 1) < HEAD_SIZE
    for a, count in enumerate(counts):
        cosine, sine = rope_angles(count, c_ref, s_ref, fc_ref, fs_ref)
        rows = slice(a * block, (a + 1) * block)
        for t in range(raw.shape[1] // 128):
            tile = raw[rows, 128 * t : 128 * t + 128]
            kv_ref[rows, 128 * t : 128 * t + 128] = jnp.where(
                low, turn(tile, cosine, sine), tile
            ).astype(BF)


def query_kernel(info_ref, normed_ref, w_ref, c_ref, s_ref, fc_ref, fs_ref, q_ref):
    block = c_ref.shape[0]
    blocks = info_ref.shape[0]
    slots = info_ref.shape[1] - 1
    raw = dot_nn(normed_ref[...], w_ref[...])
    for a in range(blocks):
        cosine, sine = rope_angles(info_ref[a, slots], c_ref, s_ref, fc_ref, fs_ref)
        rows = slice(a * block, (a + 1) * block)
        for t in range(raw.shape[1] // 128):
            tile = raw[rows, 128 * t : 128 * t + 128]
            q_ref[rows, 128 * t : 128 * t + 128] = (
                turn(tile, cosine, sine).astype(BF).astype(F32) * HEAD_SIZE**-0.5
            ).astype(BF)


def head_low(tiles, head):
    tile = tiles[:, 128 * (head // 2) : 128 * (head // 2) + 128]
    low = lax.broadcasted_iota(jnp.int32, tile.shape, 1) < HEAD_SIZE
    if head % 2:
        tile = pltpu.roll(tile, HEAD_SIZE, 1)
    return jnp.where(low, tile, jnp.zeros_like(tile))


def head_high(tiles, head):
    tile = tiles[:, 128 * (head // 2) : 128 * (head // 2) + 128]
    low = lax.broadcasted_iota(jnp.int32, tile.shape, 1) < HEAD_SIZE
    if head % 2 == 0:
        tile = pltpu.roll(tile, HEAD_SIZE, 1)
    return jnp.where(low, jnp.zeros_like(tile), tile)


def collect(info_ref, kv_ref, seen_ref, step, block, group):
    slots = info_ref.shape[1] - 1
    count = info_ref[step, slots]
    columns = slice(128 * group, 128 * group + 128)
    for m in range(slots - 1):
        source = jnp.where(m < count, info_ref[step, m], 0)
        seen_ref[m * block : (m + 1) * block] = kv_ref[
            pl.ds(pl.multiple_of(source * block, 32), block), columns
        ]
    seen_ref[(slots - 1) * block : slots * block] = kv_ref[
        pl.ds(pl.multiple_of(step * block, 32), block), columns
    ]
    if seen_ref.shape[0] > slots * block:
        seen_ref[slots * block :] = jnp.zeros_like(seen_ref[slots * block :])
    return seen_ref[...]


def seen_mask(info_ref, step, block, width):
    slots = info_ref.shape[1] - 1
    column = lax.broadcasted_iota(jnp.int32, (block, width), 1)
    row = lax.broadcasted_iota(jnp.int32, (block, width), 0)
    before = (slots - 1) * block
    return (column < info_ref[step, slots] * block) | (
        (column >= before) & (column - before <= row)
    )


def attention_kernel(
    groups, heads, info_ref, place_ref, q_ref, kv_ref, wo_ref, ctx_ref, lse_ref, kept_ref, sent_ref,
    seen_ref, out_ref,
):
    step = pl.program_id(0)
    block = q_ref.shape[0]
    per = heads // groups
    mask = seen_mask(info_ref, step, block, seen_ref.shape[0])
    mask = jnp.concatenate([mask] * per, axis=0)
    queries = q_ref[...]
    lane = lax.broadcasted_iota(jnp.int32, lse_ref.shape, 1)
    totals = jnp.zeros(lse_ref.shape, F32)
    found = []
    for g in range(groups):
        seen = collect(info_ref, kv_ref, seen_ref, step, block, g)
        packed = jnp.concatenate([head_low(queries, g * per + r) for r in range(per)], axis=0)
        scores = jnp.where(mask, dot_nt(packed, seen), -1e30)
        top = jnp.max(scores, axis=1, keepdims=True)
        shifted = jnp.exp(scores - top)
        total = jnp.sum(shifted, axis=1, keepdims=True)
        result = dot_nn(shifted.astype(BF), seen) / total
        log_total = top + jnp.log(total)
        for r in range(per):
            rows = slice(r * block, (r + 1) * block)
            found.append(result[rows])
            totals = jnp.where(lane == g * per + r, log_total[rows], totals)
    lse_ref[...] = totals
    low = lax.broadcasted_iota(jnp.int32, (block, 128), 1) < HEAD_SIZE
    tiles = []
    for t in range(ctx_ref.shape[1] // 128):
        left = pltpu.roll(found[2 * t], HEAD_SIZE, 1)
        right = found[2 * t + 1] if 2 * t + 1 < heads else jnp.zeros_like(left)
        tiles.append(jnp.where(low, left, right).astype(BF))
    context = jnp.concatenate(tiles, axis=1)
    ctx_ref[...] = context
    out_ref[pl.ds(pl.multiple_of(step * block, 32), block)] = dot_nn(context, wo_ref[...])

    @pl.when(step == pl.num_programs(0) - 1)
    def _():
        write_halves(out_ref, place_ref[2], kept_ref, sent_ref)


def attention_back_kernel(
    groups, heads, info_ref, place_ref, q_ref, kv_ref, lse_ref, g_ref, ctx_ref, n_ref, wo_ref,
    c_ref, s_ref, fc_ref, fs_ref, dq_ref, dkv_ref, kept_ref, sent_ref, seen_ref, acc_ref,
    out_grad_ref, q_grad_ref,
):
    step = pl.program_id(0)
    block = q_ref.shape[0]
    slots = info_ref.shape[1] - 1
    per = heads // groups

    @pl.when(step == 0)
    def _():
        acc_ref[...] = jnp.zeros_like(acc_ref)
        out_grad_ref[...] = jnp.zeros_like(out_grad_ref)
        q_grad_ref[...] = jnp.zeros_like(q_grad_ref)

    mask = seen_mask(info_ref, step, block, seen_ref.shape[0])
    mask = jnp.concatenate([mask] * per, axis=0)
    queries = q_ref[...]
    out_grad_ref[...] += dot_tn(ctx_ref[...], g_ref[...])
    pulled = dot_nt(g_ref[...], wo_ref[...]).astype(BF)
    lane = lax.broadcasted_iota(jnp.int32, lse_ref.shape, 1)
    count = info_ref[step, slots]
    found = []
    for g in range(groups):
        seen = collect(info_ref, kv_ref, seen_ref, step, block, g)
        packed = jnp.concatenate([head_low(queries, g * per + r) for r in range(per)], axis=0)
        grads = jnp.concatenate([head_high(pulled, g * per + r) for r in range(per)], axis=0)
        log_total = jnp.concatenate(
            [
                jnp.sum(jnp.where(lane == g * per + r, lse_ref[...], 0.0), axis=1, keepdims=True)
                for r in range(per)
            ],
            axis=0,
        )
        scores = jnp.where(mask, dot_nt(packed, seen), -1e30)
        probabilities = jnp.exp(scores - log_total)
        prob_grad = dot_nt(grads, seen)
        row_dot = jnp.sum(probabilities * prob_grad, axis=1, keepdims=True)
        score_grad = (probabilities * (prob_grad - row_dot)).astype(BF)
        query_grad = dot_nn(score_grad, seen)
        pair_grad = (dot_tn(packed, score_grad) + dot_tn(grads, probabilities.astype(BF))).T
        for r in range(per):
            found.append(query_grad[r * block : (r + 1) * block])
        columns = slice(128 * g, 128 * g + 128)
        for m in range(slots - 1):

            @pl.when(m < count)
            def _():
                rows = pl.ds(pl.multiple_of(info_ref[step, m] * block, 32), block)
                acc_ref[rows, columns] += pair_grad[m * block : (m + 1) * block]

        rows = pl.ds(pl.multiple_of(step * block, 32), block)
        acc_ref[rows, columns] += pair_grad[(slots - 1) * block : slots * block]
    cosine, sine = rope_angles(count, c_ref, s_ref, fc_ref, fs_ref)
    low = lax.broadcasted_iota(jnp.int32, (block, 128), 1) < HEAD_SIZE
    for t in range(dq_ref.shape[1] // 128):
        left = found[2 * t]
        right = (
            pltpu.roll(found[2 * t + 1], HEAD_SIZE, 1)
            if 2 * t + 1 < heads
            else jnp.zeros_like(left)
        )
        tile = jnp.where(low, left, right) * HEAD_SIZE**-0.5
        dq_ref[:, 128 * t : 128 * t + 128] = turn(tile, cosine, -sine).astype(BF)

    q_grad_ref[...] += dot_tn(dq_ref[...], n_ref[...])

    @pl.when(step == pl.num_programs(0) - 1)
    def _():
        dkv_ref[...] = acc_ref[...].astype(BF)
        rows = kept_ref.shape[0]

        @pl.when(place_ref[3] == 0)
        def _():
            kept_ref[...] = out_grad_ref[:rows].astype(BF)
            sent_ref[...] = q_grad_ref[:rows].astype(BF)

        @pl.when(place_ref[3] != 0)
        def _():
            kept_ref[...] = q_grad_ref[:rows].astype(BF)
            sent_ref[...] = out_grad_ref[:rows].astype(BF)


def project_back_kernel(info_ref, place_ref, *refs):
    *pieces, n_ref, dq_ref, wq_ref, wkv_ref, c_ref, s_ref, fc_ref, fs_ref = refs[:-7]
    kept_ref, sent_ref, kept_kv_ref, sent_kv_ref, low_ref, back_ref, grad_ref = refs[-7:]
    block = c_ref.shape[0]
    blocks = info_ref.shape[0]
    slots = info_ref.shape[1] - 1
    total = pieces[0][...].astype(F32)
    for piece in pieces[1:]:
        total = total + piece[...].astype(F32)
    low = lax.broadcasted_iota(jnp.int32, (block, 128), 1) < HEAD_SIZE
    for a in range(blocks):
        cosine, sine = rope_angles(info_ref[a, slots], c_ref, s_ref, fc_ref, fs_ref)
        rows = slice(a * block, (a + 1) * block)
        for t in range(total.shape[1] // 128):
            tile = total[rows, 128 * t : 128 * t + 128]
            low_ref[rows, 128 * t : 128 * t + 128] = jnp.where(
                low, turn(tile, cosine, -sine), tile
            ).astype(BF)
    back_ref[...] = dot_nt(dq_ref[...], wq_ref[...]) + dot_nt(low_ref[...], wkv_ref[...])
    write_halves(back_ref, place_ref[2], kept_ref, sent_ref)
    grad_ref[...] = dot_tn(low_ref[...], n_ref[...])
    share = kept_kv_ref.shape[0]
    own = pl.multiple_of(place_ref[3] * share, 8)
    other = pl.multiple_of(share - own, 8)
    kept_kv_ref[...] = grad_ref[pl.ds(own, share)].astype(BF)
    sent_kv_ref[...] = grad_ref[pl.ds(other, share)].astype(BF)


def project_key_value(zone, segments, parents, tokens, gain, weight, tables, blocks, slots):
    rows, width = tokens.shape
    whole = lambda i: (0, 0)
    operands = (tokens, gain[None], weight, *tables)
    return pl.pallas_call(
        key_value_kernel,
        grid=(1,),
        in_specs=[SMEM] * 3 + [pl.BlockSpec(o.shape, whole) for o in operands],
        out_specs=[
            pl.BlockSpec((rows, width), whole),
            pl.BlockSpec((rows, weight.shape[1]), whole),
            SMEM,
        ],
        out_shape=[
            jax.ShapeDtypeStruct((rows, width), BF),
            jax.ShapeDtypeStruct((rows, weight.shape[1]), BF),
            jax.ShapeDtypeStruct((blocks, slots + 1), jnp.int32),
        ],
        compiler_params=roomy(32),
        cost_estimate=CHEAP,
        name="project_key_value",
    )(zone, segments, parents, *operands)


def project_query(info, normed, weight, tables):
    return pl.pallas_call(
        query_kernel,
        in_specs=[SMEM] + [VMEM] * 6,
        out_specs=VMEM,
        out_shape=jax.ShapeDtypeStruct((normed.shape[0], weight.shape[1]), BF),
        compiler_params=roomy(32),
        cost_estimate=CHEAP,
        name="project_query",
    )(info, normed, weight, *tables)


def lanes_up(size):
    return -(-size // 128) * 128


def attention_forward(info, place, queries, key_value, output_weight, heads, part):
    rows, columns = queries.shape
    blocks, slots = info.shape[0], info.shape[1] - 1
    block = rows // blocks
    groups = key_value.shape[1] // 128
    width = output_weight.shape[1]
    by_block = lambda i, *_: (i, 0)
    whole = lambda i, *_: (0, 0)
    half = (rows // (2 * part), part, width)
    return pl.pallas_call(
        functools.partial(attention_kernel, groups, heads),
        grid_spec=pltpu.PrefetchScalarGridSpec(
            num_scalar_prefetch=2,
            grid=(blocks,),
            in_specs=[
                pl.BlockSpec((block, columns), by_block),
                pl.BlockSpec(key_value.shape, whole),
                pl.BlockSpec(output_weight.shape, whole),
            ],
            out_specs=[
                pl.BlockSpec((block, columns), by_block),
                pl.BlockSpec((block, 128), by_block),
                pl.BlockSpec(half, lambda i, *_: (0, 0, 0)),
                pl.BlockSpec(half, lambda i, *_: (0, 0, 0)),
            ],
            scratch_shapes=[
                pltpu.VMEM((lanes_up(slots * block), 128), BF),
                pltpu.VMEM((rows, width), F32),
            ],
        ),
        out_shape=[
            jax.ShapeDtypeStruct((rows, columns), BF),
            jax.ShapeDtypeStruct((rows, 128), F32),
            jax.ShapeDtypeStruct(half, BF),
            jax.ShapeDtypeStruct(half, BF),
        ],
        compiler_params=roomy(48),
        cost_estimate=CHEAP,
        name="attention_forward",
    )(info, place, queries, key_value, output_weight)


def attention_backward(
    info, place, queries, key_value, log_totals, branch_grad, context, normed, output_weight,
    tables, heads,
):
    rows, columns = queries.shape
    blocks, slots = info.shape[0], info.shape[1] - 1
    block = rows // blocks
    groups = key_value.shape[1] // 128
    width = output_weight.shape[1]
    by_block = lambda i, *_: (i, 0)
    whole = lambda i, *_: (0, 0)
    share = (heads * HEAD_SIZE, width)
    return pl.pallas_call(
        functools.partial(attention_back_kernel, groups, heads),
        grid_spec=pltpu.PrefetchScalarGridSpec(
            num_scalar_prefetch=2,
            grid=(blocks,),
            in_specs=[
                pl.BlockSpec((block, columns), by_block),
                pl.BlockSpec(key_value.shape, whole),
                pl.BlockSpec((block, 128), by_block),
                pl.BlockSpec((block, width), by_block),
                pl.BlockSpec((block, columns), by_block),
                pl.BlockSpec((block, width), by_block),
                pl.BlockSpec(output_weight.shape, whole),
            ]
            + [pl.BlockSpec(t.shape, whole) for t in tables],
            out_specs=[
                pl.BlockSpec((block, columns), by_block),
                pl.BlockSpec(key_value.shape, whole),
                pl.BlockSpec(share, whole),
                pl.BlockSpec(share, whole),
            ],
            scratch_shapes=[
                pltpu.VMEM((lanes_up(slots * block), 128), BF),
                pltpu.VMEM(key_value.shape, F32),
                pltpu.VMEM((columns, width), F32),
                pltpu.VMEM((columns, width), F32),
            ],
        ),
        out_shape=[
            jax.ShapeDtypeStruct((rows, columns), BF),
            jax.ShapeDtypeStruct(key_value.shape, BF),
            jax.ShapeDtypeStruct(share, BF),
            jax.ShapeDtypeStruct(share, BF),
        ],
        compiler_params=roomy(56),
        cost_estimate=CHEAP,
        name="attention_backward",
    )(info, place, queries, key_value, log_totals, branch_grad, context, normed, output_weight, *tables)


def project_backward(info, place, pieces, normed, query_low, query_weight, pair_weight, tables, part):
    rows, width = normed.shape
    columns = pair_weight.shape[1]
    half = (rows // (2 * part), part, width)
    share = (columns // 2, width)
    return pl.pallas_call(
        project_back_kernel,
        in_specs=[SMEM] * 2 + [VMEM] * (len(pieces) + 8),
        out_specs=[VMEM] * 4,
        out_shape=[jax.ShapeDtypeStruct(shape, BF) for shape in (half, half, share, share)],
        scratch_shapes=[
            pltpu.VMEM((rows, columns), BF),
            pltpu.VMEM((rows, width), F32),
            pltpu.VMEM((columns, width), F32),
        ],
        compiler_params=roomy(48),
        cost_estimate=CHEAP,
        name="project_backward",
    )(info, place, *pieces, normed, query_low, query_weight, pair_weight, *tables)


def shift(values, axis, places):
    size = lax.axis_size(axis)
    return lax.ppermute(values, axis, [(i, (i + places) % size) for i in range(size)])


def slide(values, axis, places):
    size = lax.axis_size(axis)
    return lax.ppermute(
        values, axis, [(i, i + places) for i in range(size) if 0 <= i + places < size]
    )


def swap(values, axis, bit):
    return lax.ppermute(values, axis, [(i, i ^ bit) for i in range(lax.axis_size(axis))])


def bits_of(size):
    return [1 << b for b in range(size.bit_length() - 1)]


def hold(values, *others):
    return lax.optimization_barrier((values,) + others)[0]


def halves(held, bit):
    pairs = held.reshape(held.shape[:1] + (held.shape[1] // 2, 2) + held.shape[2:])
    mine = jnp.where((lax.axis_index("tensor") & bit) != 0, 1, 0)
    return (
        lax.dynamic_index_in_dim(pairs, mine, 2, keepdims=False),
        lax.dynamic_index_in_dim(pairs, 1 - mine, 2, keepdims=False),
    )


class Line:
    def __init__(self):
        self.last = None

    def mark(self, value):
        self.last = value
        return value

    def take(self, values):
        if isinstance(values, list):
            return list(lax.optimization_barrier((*values, self.last))[:-1])
        return hold(values, self.last)

    def after(self, values, others):
        return hold(values, others)


class Gathering:
    def __init__(self, line, pieces):
        self.held = line.mark(jnp.stack(pieces)[:, None])
        self.bits = bits_of(lax.axis_size("tensor"))[::-1]
        self.send(line)

    def send(self, line):
        if self.bits:
            self.coming = swap(self.held, "tensor", self.bits[0])

    def step(self, line):
        other = line.take(self.coming)
        mine = (lax.axis_index("tensor") & self.bits[0]) != 0
        held = jnp.where(
            mine, jnp.stack([other, self.held], axis=2), jnp.stack([self.held, other], axis=2)
        )
        self.held = line.mark(held.reshape((held.shape[0], -1) + held.shape[3:]))
        self.bits = self.bits[1:]
        self.send(line)

    def rows(self):
        return self.held.reshape(-1, self.held.shape[-1])


class Summing:
    def __init__(self, line, rows=None, split=None):
        size = lax.axis_size("tensor")
        self.bits = bits_of(size)
        if split is None:
            self.held = rows.reshape((rows.shape[0], size, -1) + rows.shape[2:])
            self.send(line)
        else:
            self.kept, sent = split
            self.coming = swap(line.take(sent), "tensor", self.bits[0])

    def send(self, line):
        if self.bits:
            self.kept, sent = halves(self.held, self.bits[0])
            self.coming = swap(line.mark(sent), "tensor", self.bits[0])

    def step(self, line):
        coming = line.take(self.coming)
        self.held = line.mark((self.kept.astype(F32) + coming.astype(F32)).astype(BF))
        self.bits = self.bits[1:]
        self.send(line)


class Mixing:
    def __init__(self, line, groups, part):
        self.bits = bits_of(lax.axis_size("tensor"))
        both = [halves(g.reshape(1, -1, part, g.shape[1]), self.bits[0]) for g in groups]
        self.kept = jnp.concatenate([b[0] for b in both], axis=0)
        sent = line.mark(jnp.concatenate([b[1] for b in both], axis=0))
        self.coming = swap(sent, "tensor", self.bits[0])

    def step(self, line):
        coming = line.take(self.coming)
        self.held = line.mark((self.kept.astype(F32) + coming.astype(F32)).astype(BF))
        self.bits = self.bits[1:]
        if self.bits:
            self.kept, sent = halves(self.held, self.bits[0])
            self.coming = swap(line.mark(sent), "tensor", self.bits[0])

    def homes(self, line):
        groups = line.take(self.held[:, 0])
        size = groups.shape[0]
        return [groups[0]] + [shift(groups[k], "expert", size - k) for k in range(1, size)]


class Exchange:
    def __init__(self, line, half, up_shape, down_shape):
        self.line, self.half, self.shapes = line, half, (up_shape, down_shape)
        self.waiting, self.flying, self.landed, self.totals = [], None, [], None
        self.done = 0

    def add(self, grads):
        self.waiting.append(grads)
        if self.flying is None:
            self.begin()

    def begin(self):
        grads = self.line.take(self.waiting.pop(0))
        self.flying = lax.all_gather(grads, "dp", axis=0, tiled=True)

    def land(self):
        if self.flying is not None:
            self.landed.append(self.line.mark(self.line.take(self.flying)))
            self.flying = None
            if self.waiting:
                self.begin()

    def settle(self):
        while self.landed:
            grads = self.line.take(self.landed.pop(0))
            self.totals = finish_weights(grads, self.totals, self.done, self.half, *self.shapes)
            self.line.mark(self.totals[1])
            self.done += grads.shape[0] // 2


class AllSum:
    def __init__(self, line, kept, sent):
        self.kept = kept
        self.size = lax.axis_size("expert")
        self.coming = swap(line.take(sent), "dp", 1)
        self.stage = 0

    def spread(self, blocks):
        return lax.all_to_all(blocks, "expert", split_axis=0, concat_axis=0)

    def step(self, line):
        coming = line.take(self.coming)
        if self.stage == 0:
            both = line.mark((self.kept.astype(F32) + coming.astype(F32)).astype(BF))
            self.coming = self.spread(both.reshape((self.size, -1) + both.shape[1:]))
        elif self.stage == 1:
            total = coming[0].astype(F32)
            for k in range(1, self.size):
                total = total + coming[k].astype(F32)
            own = line.mark(jnp.broadcast_to(total.astype(BF)[None], coming.shape))
            self.coming = self.spread(own)
        elif self.stage == 2:
            self.own = line.mark(coming.reshape(self.kept.shape))
            self.coming = swap(self.own, "dp", 1)
        else:
            first = lax.axis_index("dp") == 0
            self.shares = (
                jnp.where(first, self.own, coming).astype(F32),
                jnp.where(first, coming, self.own).astype(F32),
            )
            line.mark(self.shares[0])
        self.stage += 1


class SmallSum:
    def __init__(self, line, values):
        self.values = values
        self.coming = swap(line.take(values), "dp", 1)
        self.stage = 0

    def step(self, line):
        coming = line.take(self.coming)
        if self.stage == 0:
            both = self.values + coming
            size = lax.axis_size("expert")
            own = line.mark(jnp.broadcast_to(both[None], (size,) + both.shape))
            self.coming = lax.all_to_all(own, "expert", split_axis=0, concat_axis=0)
        else:
            self.values = line.mark(jnp.sum(coming, axis=0))
        self.stage += 1


def shards(
    tokens,
    out_cotangent,
    first_gain,
    query_weight,
    key_value_matrix,
    output_weight,
    second_gain,
    expert_gate_up,
    expert_down,
    routes,
    route_gates,
    expert_slot,
    parent_segments,
    token_segments,
):
    row_count, width = tokens.shape
    tree_rows = token_segments.shape[0]
    query_columns = query_weight.shape[1]
    heads = query_columns // HEAD_SIZE
    local_experts = expert_gate_up.shape[0]
    all_experts = expert_slot.shape[0]
    devices = lax.axis_size("expert")
    zone = lax.axis_index("expert")
    tensor_bits = bits_of(lax.axis_size("tensor"))
    core = lax.axis_index("tensor") % 2
    part = row_count // lax.axis_size("tensor")
    first_part = lax.axis_index("tensor") * part
    leaf = tree_rows // 12
    block = math.gcd(leaf, row_count)
    blocks = row_count // block
    slots = 7 * leaf // block
    tables = rope_tables(block, slots)
    if query_columns % 128:
        query_weight = jnp.pad(query_weight, ((0, 0), (0, HEAD_SIZE)))
        output_weight = jnp.pad(output_weight, ((0, HEAD_SIZE), (0, 0)))

    normed_one, key_value, info = project_key_value(
        zone[None].astype(jnp.int32), token_segments, parent_segments, tokens, first_gain,
        key_value_matrix, tables, blocks, slots,
    )
    key_values = [key_value] + [slide(key_value, "expert", k) for k in range(1, devices)]
    queries = project_query(info, normed_one, query_weight, tables)
    experts_range = jnp.arange(all_experts, dtype=jnp.int32)[None, None, :]
    routed = jnp.sum(
        jnp.where(routes[:, :, None] == experts_range, expert_slot[None, None, :], 0), axis=2
    )
    dense = jnp.sum(
        jnp.where(routed[:, :, None] == experts_range, route_gates[:, :, None], 0.0), axis=1
    )
    dense_high = lax.reduce_precision(dense, 8, 7)
    own_gates = jnp.concatenate(
        [
            dense_high.astype(BF),
            (dense - dense_high).astype(BF),
            jnp.zeros((row_count, 128 - 2 * all_experts), BF),
        ],
        axis=1,
    )
    cotangent_part = lax.dynamic_slice_in_dim(out_cotangent, first_part, part, 0)
    gates_part = lax.dynamic_slice_in_dim(own_gates, first_part, part, 0)
    all_cotangents = lax.all_gather(
        jnp.concatenate([cotangent_part, gates_part], axis=1),
        ("dp", "expert", "tensor"),
        axis=0,
        tiled=True,
    )
    line = Line()
    line.mark(queries)
    key_values = line.mark(jnp.concatenate(line.take(key_values), axis=0))
    tree = lax.axis_index("dp")
    places = [
        jnp.stack(
            [tree * devices + (zone - k) % devices, zone * local_experts, core, tree, zone]
        ).astype(jnp.int32)
        for k in range(devices)
    ]
    context, log_totals, *split = attention_forward(
        info, places[0], queries, key_values, output_weight, heads, part
    )
    line.mark(context)
    summing = Summing(line, split=[h[None] for h in split])
    while summing.bits:
        summing.step(line)
    attention = summing.held[0, 0].astype(F32)
    inputs_part = lax.dynamic_slice_in_dim(tokens, first_part, part, 0).astype(F32)
    hidden_state = inputs_part + attention
    second_float = second_gain.astype(F32)
    normed_two = line.mark(normalize(hidden_state, second_float).astype(BF))

    gate_up, down = expert_gate_up, expert_down
    if gate_up.shape[2] == 2 * PAIR:
        gate_up = jnp.pad(gate_up, ((0, 0), (0, 0), (0, 2 * PAIR)))
        down = jnp.pad(down, ((0, 0), (0, PAIR), (0, 0)))
    if local_experts % 2:
        gate_up = jnp.pad(gate_up, ((0, 1), (0, 0), (0, 0)))
        down = jnp.pad(down, ((0, 1), (0, 0), (0, 0)))
    experts = gate_up.shape[0]
    half = experts // 2
    cots = [Rows(out_cotangent, 0)] + [Rows(all_cotangents) for _ in range(1, devices)]
    gates = [(Rows(own_gates, 0), 0)] + [(Rows(all_cotangents), width // 128)] * (devices - 1)
    xs = [None] * devices
    mains = [None] * devices
    running, homes = [], []
    total = None

    def advance(total):
        while homes:
            home = line.mark(line.take(homes.pop(0))).astype(F32)
            total = home if total is None else total + home
        for k, summing in list(running):
            summing.step(line)
            if not summing.bits:
                running.remove((k, summing))
                own = line.take(summing.held[0, 0])
                homes.append(shift(own, "expert", devices - k) if k else own)
        return total

    def run_main(k, total):
        mains[k] = experts_main(
            places[k], Rows(line.take(xs[k].array), xs[k].index), cots[k], *gates[k], gate_up,
            down, row_count, all_experts, part,
        )
        line.mark(mains[k][2])
        total = advance(total)
        running.append((k, Summing(line, split=[h[None] for h in mains[k][2:]])))
        return total

    nearest = shift(normed_two, "expert", 1)
    own_rows = Gathering(line, [normed_two])
    other_part = swap(normed_two, "dp", 1)
    nearest = line.mark(line.take(nearest))
    near_rows = Gathering(line, [nearest])
    own_rows.step(line)
    others = [shift(line.take(normed_two), "expert", k) for k in range(2, devices)]
    while own_rows.bits:
        own_rows.step(line)
    xs[0] = Rows(own_rows.rows(), 0)
    total = run_main(0, total)
    other_part = line.mark(line.take(other_part))
    x_other = lax.all_gather(other_part, ("expert", "tensor"), axis=0, tiled=True)
    near_rows.step(line)
    far = []
    for k in range(2, devices, 2):
        far.append(Gathering(line, line.take(others[k - 2 : k])))
    while near_rows.bits:
        near_rows.step(line)
    xs[1] = Rows(near_rows.rows(), 0)
    total = run_main(1, total)
    for n, gathering in enumerate(far):
        while gathering.bits:
            gathering.step(line)
            total = advance(total)
        rows = gathering.rows()
        for j in range(2):
            xs[2 + 2 * n + j] = Rows(rows, j)
            total = run_main(2 + 2 * n + j, total)
    hidden_grads, activations = [k[1] for k in mains], [k[0] for k in mains]
    flat_down = down.reshape(-1, width)
    mixed = []
    while running or homes:
        if len(mixed) < devices:
            array = line.take(activations[len(mixed)])
            mixed.append(
                line.mark(jnp.dot(array, flat_down, preferred_element_type=F32).astype(BF))
            )
        total = advance(total)
    while len(mixed) < devices:
        array = line.take(activations[len(mixed)])
        mixed.append(line.mark(jnp.dot(array, flat_down, preferred_element_type=F32).astype(BF)))
    normed_two_grad = total
    _, norm_two_pull = jax.vjp(normalize, hidden_state, second_float)
    hidden_norm_grad, second_gain_grad = norm_two_pull(normed_two_grad)
    residual_grad = line.mark(cotangent_part.astype(F32) + hidden_norm_grad)

    gathering = Gathering(line, [residual_grad.astype(BF)])
    mixing = Mixing(line, line.take(mixed), part)
    ga_other, hg_other = experts_other(
        places[0], line.take(x_other), all_cotangents, gate_up, down, row_count, all_experts
    )
    line.mark(ga_other)

    def weight_grads(first, count):
        x_late = line.take(x_other)
        groups = [
            (xs[k].array, hidden_grads[k], activations[k], xs[k].index, 0, k, devices)
            for k in range(devices)
        ] + [(x_late, hg_other, ga_other, k, k, None, devices) for k in range(devices)]
        parts = [
            experts_weights(
                places[0], groups[g : g + 8], all_cotangents, first, count, half, row_count
            )
            for g in range(0, len(groups), 8)
        ]
        if len(parts) == 1:
            return parts[0]
        return sum(p.astype(F32) for p in parts).astype(BF)

    exchange = Exchange(line, half, expert_gate_up.shape, expert_down.shape)
    split_count = (half + 1) // 2
    gathering.step(line)
    mixing.step(line)
    while gathering.bits:
        gathering.step(line)
    branch_grad = line.mark(gathering.rows())
    query_low, pair_all, *split = attention_backward(
        info, places[0], queries, key_values, log_totals, line.take(branch_grad), context,
        normed_one, output_weight, tables, heads,
    )
    line.mark(query_low)
    pieces = line.take(pair_all).reshape(devices, row_count, pair_all.shape[1])
    pieces = [pieces[0]] + [slide(pieces[k], "expert", -k) for k in range(1, devices)]
    outer_sum = AllSum(line, *split)
    first_grads = line.mark(weight_grads(0, split_count))
    outer_sum.step(line)
    pieces = line.take(pieces)
    line.mark(pieces[1])
    exchange.add(first_grads)
    *split, pair_kept, pair_sent = project_backward(
        info, places[0], pieces, normed_one, query_low, query_weight, key_value_matrix, tables,
        part,
    )
    line.mark(pair_kept)
    summing = Summing(line, split=[h[None] for h in split])
    pair_sum = AllSum(line, pair_kept, pair_sent)
    summing.step(line)
    last_grads = line.mark(weight_grads(split_count, half - split_count))
    while summing.bits:
        summing.step(line)
    outer_sum.step(line)
    pair_sum.step(line)
    while mixing.bits:
        mixing.step(line)
    normed_one_grad = summing.held[0, 0].astype(F32)
    _, norm_one_pull = jax.vjp(normalize, inputs_part, first_gain.astype(F32))
    input_norm_grad, first_gain_grad = norm_one_pull(normed_one_grad)
    input_part = line.mark((residual_grad + input_norm_grad).astype(BF))
    extra = jnp.zeros((8, width), F32).at[0].set(first_gain_grad).at[1].set(second_gain_grad)
    gathering = Gathering(line, [jnp.concatenate([input_part, extra.astype(BF)], axis=0)])
    homes = mixing.homes(line)
    exchange.add(last_grads)
    gathering.step(line)
    outer_sum.step(line)
    pair_sum.step(line)
    while gathering.bits:
        gathering.step(line)
    exchange.land()
    rows = gathering.held.reshape(-1, part + 8, width)
    input_gradient = rows[:, :part].reshape(row_count, width)
    gains = SmallSum(line, jnp.sum(rows[:, part:].astype(F32), axis=0))
    mixture = homes[0].astype(F32)
    for home in homes[1:]:
        mixture = mixture + line.take(home).astype(F32)
    gathering = Gathering(line, [line.mark((hidden_state + mixture).astype(BF))])
    pair_sum.step(line)
    gains.step(line)
    outer_sum.step(line)
    gathering.step(line)
    while gathering.bits:
        gathering.step(line)
    layer_output = gathering.rows()
    pair_sum.step(line)
    exchange.settle()
    gains.step(line)
    gains = gains.values
    while exchange.flying is not None:
        exchange.land()
        exchange.settle()
    totals = exchange.totals
    return (
        layer_output,
        input_gradient,
        gains[0],
        outer_sum.shares[1].T,
        jnp.concatenate(pair_sum.shares, axis=0).T,
        outer_sum.shares[0],
        gains[1],
        *totals,
    )


def solution(mesh):
    in_specs = (
        P(("dp", "expert"), None),
        P(("dp", "expert"), None),
        P(),
        P(None, "tensor"),
        P(None, "tensor"),
        P("tensor", None),
        P(),
        P("expert", None, "tensor"),
        P("expert", "tensor", None),
        P(("dp", "expert"), None),
        P(("dp", "expert"), None),
        P(),
        P("dp", None),
        P("dp"),
    )
    out_specs = (
        P(("dp", "expert"), None),
        P(("dp", "expert"), None),
        P(),
        P(None, "tensor"),
        P(None, "tensor"),
        P("tensor", None),
        P(),
        P("expert", None, "tensor"),
        P("expert", "tensor", None),
    )
    return jax.shard_map(shards, mesh=mesh, in_specs=in_specs, out_specs=out_specs, check_vma=False)
```
